32 devices in a mesh: tile: 4 (over y, x), src: 8 (over z, core).
Axes of the slice: x: 2, y: 2, z: 4, core: 2. Of those that a mesh axis runs over, the one named last changes fastest.
Arguments:
- log_conductivity: float32 [32, 8, 512], P('src', None, 'tile'), may hold values from -1 to 1
- cluster_labels: int32 [32, 8, 512], P('src', None, 'tile'), may hold values from 0 to 3
- cluster_means: float32 [4], replicated, may hold values from -1 to 1
- cluster_vars: float32 [4], replicated, may hold values from 0.25 to 1
- source_cells: int32 [8, 2], P('src'), may hold values from 0 to 131071
- receiver_cells: int32 [256, 2], replicated, may hold values from 0 to 131071
- observed: float32 [8, 256], P('src'), may hold values from -6 to 6
- warm_potential: float32 [8, 32, 8, 512], P('src', None, None, 'tile'), may hold values from -6 to 6
- warm_adjoint: float32 [8, 32, 8, 512], P('src', None, None, 'tile'), may hold values from -6 to 6
Outputs:
- potentials: float32 [8, 32, 8, 512], P('src', None, None, 'tile')
- adjoints: float32 [8, 32, 8, 512], P('src', None, None, 'tile')
- misfit: float32 [8, 256], P('src')
- gradient: float32 [32, 8, 512], P('src', None, 'tile')
The draws below stay inside these ranges and needn't reach their ends.
Inputs may be any that keep to these rules, and one draw needn't show every extreme that they name: `source_cells`: flat cell indices. `receiver_cells`: flat cell indices.
All inputs are finite; a program needn't handle non-finite values.
Results may differ from the reference program's by a relative error of at most 0.0003.
Values sent between devices are 32-bit elements; how exact they have to be, the bound alone decides.
No kernel may reach another device: no remote copies, remote signals or barrier semaphores. Data moves between devices by JAX's collectives and lax.ppermute only.
A program may use at most 64 MiB of HBM per device.

```python
import math
import jax
import jax.numpy as jnp
from jax import lax

NY = 32
NZ = 8
RECEIVERS = 256
SWEEPS = 8
CLUSTERS = 4
NX = 512
SOURCES = 8
CELLS = 131072


def touch_ends(array, own_key, low, high):
    extent = array.shape
    spot = [jax.random.randint(jax.random.fold_in(own_key, axis), (), 0, extent[axis]) for axis in range(len(extent))]
    array = array.at[tuple(spot)].set(low)
    longest = extent.index(max(extent))
    spot[longest] = (spot[longest] + 1) % extent[longest]
    return array.at[tuple(spot)].set(high)


def steps_of(rng, extent, shards, smallest, largest):
    factor_of = 1.0
    for axis_at, parts in shards:
        heights = jax.random.uniform(jax.random.fold_in(jax.random.fold_in(rng, 6), axis_at), (parts,), jnp.float32, smallest / len(shards), largest / len(shards))
        factor_of = factor_of * jnp.repeat(jnp.exp(heights), extent[axis_at] // parts).reshape((-1,) + (1,) * (len(extent) - 1 - axis_at))
    return factor_of


def bell_draw(stream_key, shape, width, reach, cuts=(), kind=jnp.bfloat16):
    gain = steps_of(stream_key, shape, cuts, -0.22, 0.18) if cuts else 1.0
    entries = jax.random.normal(stream_key, shape, jnp.float32) * width * gain
    return jnp.minimum(jnp.maximum(entries, -reach), reach).astype(kind)


def setup_inputs(seed: int = 0) -> dict:
    splits = jax.random.split(jax.random.key(seed), 10)
    log_conductivity = jnp.clip(jax.random.uniform(splits[0], (NY, NZ, NX), jnp.float32, -1.0, 1.0) * steps_of(splits[0], (NY, NZ, NX), ((0, 8), (2, 4)), -0.4, 0.0), -1.0, 1.0)
    cluster_labels = touch_ends(jax.random.randint(splits[1], (NY, NZ, NX), 0, CLUSTERS), jax.random.fold_in(splits[1], 1), 0, CLUSTERS - 1).astype(jnp.int32)
    cluster_means = jnp.clip(jax.random.uniform(splits[2], (CLUSTERS,), jnp.float32, -1.0, 1.0), -1.0, 1.0)
    cluster_vars = jnp.clip(jnp.exp(jax.random.uniform(splits[3], (CLUSTERS,), jnp.float32, math.log(0.25), math.log(1.0))), 0.25, 1.0)
    source_cells = touch_ends(jax.random.randint(splits[4], (SOURCES, 2), 0, CELLS), jax.random.fold_in(splits[4], 1), 0, CELLS - 1).astype(jnp.int32)
    receiver_cells = touch_ends(jax.random.randint(splits[5], (RECEIVERS, 2), 0, CELLS), jax.random.fold_in(splits[5], 1), 0, CELLS - 1).astype(jnp.int32)
    observed = bell_draw(splits[6], (SOURCES, RECEIVERS), 1.0, 6.0, ((0, 8),), jnp.float32)
    warm_potential = bell_draw(splits[7], (SOURCES, NY, NZ, NX), 1.0, 6.0, ((0, 8), (3, 4)), jnp.float32)
    warm_adjoint = bell_draw(splits[8], (SOURCES, NY, NZ, NX), 1.0, 6.0, ((0, 8), (3, 4)), jnp.float32)
    return {"log_conductivity": log_conductivity, "cluster_labels": cluster_labels, "cluster_means": cluster_means, "cluster_vars": cluster_vars, "source_cells": source_cells, "receiver_cells": receiver_cells, "observed": observed, "warm_potential": warm_potential, "warm_adjoint": warm_adjoint}


LEAKAGE = 0.05
WEIGHT_X = 1.0
WEIGHT_Y = 0.5
WEIGHT_Z = 0.5
SMALLNESS = 1.0


def shift_down(values, along):
    length = values.shape[along]
    zero_slab = jnp.zeros_like(lax.slice_in_dim(values, 0, 1, axis=along))
    return jnp.concatenate([zero_slab, lax.slice_in_dim(values, 0, length - 1, axis=along)], axis=along)


def shift_up(values, along):
    length = values.shape[along]
    zero_slab = jnp.zeros_like(lax.slice_in_dim(values, 0, 1, axis=along))
    return jnp.concatenate([lax.slice_in_dim(values, 1, length, axis=along), zero_slab], axis=along)


def face_pair(first, second, along):
    length = first.shape[along]
    product = (lax.slice_in_dim(first, 1, length, axis=along) - lax.slice_in_dim(first, 0, length - 1, axis=along)) * (
        lax.slice_in_dim(second, 1, length, axis=along) - lax.slice_in_dim(second, 0, length - 1, axis=along))
    zero_slab = jnp.zeros_like(lax.slice_in_dim(product, 0, 1, axis=along))
    return jnp.concatenate([zero_slab, product], axis=along) + jnp.concatenate([product, zero_slab], axis=along)


def coefficients(sigma):
    def faces_along(along, weight):
        length = sigma.shape[along]
        inside = weight * 0.5 * (lax.slice_in_dim(sigma, 0, length - 1, axis=along) + lax.slice_in_dim(sigma, 1, length, axis=along))
        zero_slab = jnp.zeros_like(lax.slice_in_dim(sigma, 0, 1, axis=along))
        return jnp.concatenate([inside, zero_slab], axis=along)

    right_x = faces_along(2, WEIGHT_X)
    left_x = shift_down(right_x, 2)
    next_y = faces_along(0, WEIGHT_Y)
    prev_y = shift_down(next_y, 0)
    next_z = faces_along(1, WEIGHT_Z)
    prev_z = shift_down(next_z, 1)
    diagonal = (left_x + right_x + next_y + next_z + prev_z + LEAKAGE * sigma) + prev_y
    return (left_x, right_x, next_y, prev_y, next_z, prev_z, diagonal)


def relax_step(field, source_term, coefs):
    left_x, right_x, next_y, prev_y, next_z, prev_z, diagonal = coefs
    neighbours = left_x * shift_down(field, 2) + right_x * shift_up(field, 2)
    neighbours = neighbours + prev_y * shift_down(field, 0) + next_y * shift_up(field, 0)
    neighbours = neighbours + prev_z * shift_down(field, 1) + next_z * shift_up(field, 1)
    return (source_term + neighbours) / diagonal


def products(field, adjoint):
    paired = WEIGHT_X * face_pair(field, adjoint, 2) + WEIGHT_Y * face_pair(field, adjoint, 0) + WEIGHT_Z * face_pair(field, adjoint, 1)
    return 0.5 * paired + LEAKAGE * field * adjoint


def reference(log_conductivity, cluster_labels, cluster_means, cluster_vars, source_cells, receiver_cells, observed, warm_potential, warm_adjoint):
    sigma = jnp.exp(log_conductivity)
    coefs = coefficients(sigma)
    shape = log_conductivity.shape
    cell_index = (lax.broadcasted_iota(jnp.int32, shape, 0) * shape[1] + lax.broadcasted_iota(jnp.int32, shape, 1)) * shape[2] + lax.broadcasted_iota(jnp.int32, shape, 2)
    first_rx = receiver_cells[:, 0]
    second_rx = receiver_cells[:, 1]

    def one_source(total, inputs):
        electrodes, observed_row, start_field, start_adjoint = inputs
        source_term = (cell_index == electrodes[0]).astype(jnp.float32) - (cell_index == electrodes[1]).astype(jnp.float32)
        field = start_field
        for sweep_index in range(SWEEPS):
            field = relax_step(field, source_term, coefs)
        flat_field = field.reshape(-1)
        residual = flat_field[first_rx] - flat_field[second_rx] - observed_row
        adjoint_source = jnp.zeros(flat_field.shape, jnp.float32).at[first_rx].add(residual).at[second_rx].add(-residual).reshape(shape)
        adjoint = start_adjoint
        for sweep_index in range(SWEEPS):
            adjoint = relax_step(adjoint, adjoint_source, coefs)
        return total + products(field, adjoint), (field, adjoint, residual)

    total, (fields, adjoints, residuals) = lax.scan(one_source, jnp.zeros(shape, jnp.float32), (source_cells, observed, warm_potential, warm_adjoint))
    mean_cell = jnp.zeros(shape, jnp.float32)
    var_cell = jnp.zeros(shape, jnp.float32)
    for cluster in range(CLUSTERS):
        mean_cell = mean_cell + jnp.where(cluster_labels == cluster, cluster_means[cluster], 0.0)
        var_cell = var_cell + jnp.where(cluster_labels == cluster, cluster_vars[cluster], 0.0)
    gradient = -sigma * total + SMALLNESS * (log_conductivity - mean_cell) / var_cell
    return (fields, adjoints, residuals, gradient)
```

```python
import functools

import jax
import jax.numpy as jnp
from jax import lax
from jax.experimental import pallas as pl
from jax.experimental.pallas import tpu as pltpu
from jax.sharding import PartitionSpec as P

SWEEPS = 8
CLUSTERS = 4
HALO = SWEEPS + 1

LEAKAGE = 0.05
WEIGHT_X = 1.0
WEIGHT_Y = 0.5
WEIGHT_Z = 0.5
SMALLNESS = 1.0

F32 = jnp.float32
BF16 = jnp.bfloat16
VMEM = pl.BlockSpec(memory_space=pltpu.VMEM)
SMEM = pl.BlockSpec(memory_space=pltpu.SMEM)
PARAMS = pltpu.CompilerParams(vmem_limit_bytes=24 * 1024 * 1024)


def xor_pairs(count, bit):
    return [(i, i ^ bit) for i in range(count)]


def lanes(shape):
    return lax.broadcasted_iota(jnp.int32, shape, len(shape) - 1)


def wide_columns(shape):
    lane = lanes(shape)
    width = shape[-1]
    return jnp.where(lane < width - width // 4, lane, lane - width)


def turn(values, shift):
    return pltpu.roll(values, shift % values.shape[-1], values.ndim - 1)


def pack_kernel(order, info, gathered, own_v, own_a, other_v, other_a, payload, model):
    peers, rows_own = gathered.shape[:2]
    rows = model.shape[0]
    half = rows // 2
    me, right = info[0], info[1]
    for i in range(peers):
        j = sum(((i >> n) & 1) << bit for n, bit in enumerate(order))
        model[pl.ds((me ^ j) * rows_own, rows_own)] = gathered[i]
    lane = lanes((8, 128))

    def fill(start):
        sources = (own_v, own_a, model, other_v, other_a, model)
        for row in range(half):
            out = jnp.zeros((8, 128), F32)
            for group in range(2):
                for k, ref in enumerate(sources):
                    place = 64 * group + HALO * k
                    piece = turn(ref[row + half * group], place - start)
                    out = jnp.where((lane >= place) & (lane < place + HALO), piece, out)
            payload[row] = out

    @pl.when(right == 1)
    def _():
        fill(128 - HALO)

    @pl.when(right == 0)
    def _():
        fill(0)


def side_buffers(right, mine, theirs, row):
    near = mine[row]
    far = turn(theirs[row], -3 * HALO)
    on_right = jnp.full((8, 128), right, jnp.int32) == 1
    return jnp.where(on_right, near, far), jnp.where(on_right, far, near)


def halo_row(after, before, base, slot):
    lane = lanes((8, 128))
    first = turn(after, -(base + HALO * slot))
    last = turn(before, 128 - HALO - base - HALO * slot)
    return jnp.where(lane < HALO, first, jnp.where(lane >= 128 - HALO, last, 0.0))


def sweep(source, target, right_side, fx, fy, fz, inverse):
    rows = source.shape[0]
    for y in range(rows):
        v = source[y]
        face_x = fx[y]
        face_z = fz[y]
        total = right_side[y] + face_x * turn(v, -1) + turn(face_x * v, 1)
        total = total + (face_z * pltpu.roll(v, 7, 0) + pltpu.roll(face_z * v, 1, 0))
        if y + 1 < rows:
            total = total + fy[y] * source[y + 1]
        if y > 0:
            total = total + fy[y - 1] * source[y - 1]
        target[y] = total * inverse[y]


def relax(first, second, right_side, fx, fy, fz, inverse):
    def two(_, carry):
        sweep(first, second, right_side, fx, fy, fz, inverse)
        sweep(second, first, right_side, fx, fy, fz, inverse)
        return carry

    lax.fori_loop(0, SWEEPS // 2, two, 0)


def three_parts(values):
    high = values.astype(BF16)
    rest = values - high.astype(F32)
    middle = rest.astype(BF16)
    low = (rest - middle.astype(F32)).astype(BF16)
    return high, middle, low


def field_kernel(
    total_x, info, cells, model, mine, theirs, warm, spots,
    field_out, picked, wide, fx, fy, fz, inverse, other, right_side,
):
    rows, depth, width = model.shape
    span = 2 * width
    half = rows // 2
    right, first_col = info[1], info[2]
    col = first_col + wide_columns((depth, span))
    depth_at = lax.broadcasted_iota(jnp.int32, (depth, span), 0)
    closed_x = (col == total_x - 1) | (col == -1)
    wide_sigma = other
    for row in range(half):
        after, before = side_buffers(right, mine, theirs, row)
        for group in range(2):
            y = row + half * group
            wide[y, :, :width] = warm[y]
            wide[y, :, width:] = halo_row(after, before, 64 * group, 0)
            wide_sigma[y, :, :width] = jnp.exp(model[y])
            wide_sigma[y, :, width:] = jnp.exp(halo_row(after, before, 64 * group, 2))
    previous = jnp.zeros((depth, span), F32)
    for y in range(rows):
        s = wide_sigma[y]
        face_x = jnp.where(closed_x, 0.0, WEIGHT_X * 0.5 * (s + turn(s, -1)))
        face_z = jnp.where(depth_at == depth - 1, 0.0, WEIGHT_Z * 0.5 * (s + pltpu.roll(s, depth - 1, 0)))
        if y + 1 < rows:
            face_y = WEIGHT_Y * 0.5 * (s + wide_sigma[y + 1])
        else:
            face_y = jnp.zeros((depth, span), F32)
        diagonal = face_x + turn(face_x, 1) + face_z + pltpu.roll(face_z, 1, 0) + LEAKAGE * s + face_y + previous
        fx[y] = face_x
        fy[y] = face_y
        fz[y] = face_z
        inverse[y] = 1.0 / diagonal
        previous = face_y
        right_side[y] = jnp.zeros((depth, span), F32)
    for k, sign in ((0, 1.0), (1, -1.0)):
        cell = cells[0, k]
        line = cell // total_x
        y = line // depth
        hit = (col == cell - line * total_x) & (depth_at == line - y * depth)
        right_side[y] = right_side[y] + jnp.where(hit, sign, 0.0)
    relax(wide, other, right_side, fx, fy, fz, inverse)
    field = wide[:, :, :width]
    field_out[0] = field
    count = spots.shape[1]
    x_row = spots[0:1, :] - first_col
    line_row = spots[1:2, :]
    hit_x = jnp.where(lax.broadcasted_iota(jnp.int32, (width, count), 0) == x_row, 1.0, 0.0).astype(BF16)
    flat = field.reshape(rows * depth, width)
    lines = sum(jnp.dot(part, hit_x, preferred_element_type=F32) for part in three_parts(flat))
    hit_line = lax.broadcasted_iota(jnp.int32, (rows * depth, count), 0) == line_row
    got = jnp.sum(jnp.where(hit_line, lines, 0.0), axis=0, keepdims=True)
    picked[...] = got[:, : count // 2] - got[:, count // 2 :]


def adjoint_kernel(
    total_x, places, info, picked, observed, spots, mine, theirs, warm, wide_v, fx, fy, fz, inverse,
    adjoint_out, misfit_out, terms, wide, other, right_side,
):
    rows, depth, span = wide_v.shape
    width = span // 2
    half = rows // 2
    me, right, first_col = info[0], info[1], info[2]
    count = spots.shape[1]
    col = first_col + wide_columns((depth, span))
    misfit = picked[...] - observed[...]
    misfit_out[...] = misfit
    weights = jnp.concatenate([misfit, -misfit], axis=1)
    hit_line = lax.broadcasted_iota(jnp.int32, (rows * depth, count), 0) == spots[1:2, :]
    at = lax.broadcasted_iota(jnp.int32, (span, count), 0)
    at = first_col + jnp.where(at < span - span // 4, at, at - span)
    hit_x = jnp.where(at == spots[0:1, :], 1.0, 0.0).astype(BF16)
    flat = jnp.zeros((rows * depth, span), F32)
    for part in three_parts(weights):
        left = jnp.where(hit_line, part.astype(F32), 0.0).astype(BF16)
        flat = flat + lax.dot_general(left, hit_x, (((1,), (1,)), ((), ())), preferred_element_type=F32)
    right_side[...] = flat.reshape(rows, depth, span)
    for row in range(half):
        after, before = side_buffers(right, mine, theirs, row)
        for group in range(2):
            y = row + half * group
            wide[y, :, :width] = warm[y]
            wide[y, :, width:] = halo_row(after, before, 64 * group, 1)
    relax(wide, other, right_side, fx, fy, fz, inverse)
    adjoint_out[0] = wide[:, :, :width]
    closed_x = (col == total_x - 1) | (col == -1)
    depth_at = lax.broadcasted_iota(jnp.int32, (depth, width), 0)
    peers, rows_own = terms.shape[:2]
    py_prev = jnp.zeros((depth, width), F32)
    for y in range(rows):
        f, a = wide_v[y], wide[y]
        px = jnp.where(closed_x, 0.0, (turn(f, -1) - f) * (turn(a, -1) - a))
        px = (px + turn(px, 1))[:, :width]
        f, a = f[:, :width], a[:, :width]
        pz = (pltpu.roll(f, depth - 1, 0) - f) * (pltpu.roll(a, depth - 1, 0) - a)
        pz = jnp.where(depth_at == depth - 1, 0.0, pz)
        pz = pz + pltpu.roll(pz, 1, 0)
        if y + 1 < rows:
            py = (wide_v[y + 1, :, :width] - f) * (wide[y + 1, :, :width] - a)
        else:
            py = jnp.zeros((depth, width), F32)
        paired = WEIGHT_X * px + WEIGHT_Y * (py_prev + py) + WEIGHT_Z * pz
        py_prev = py
        j = me ^ (y // rows_own)
        place = sum(((j >> bit) & 1) << n for n, bit in enumerate(reversed(places)))
        terms[place, y % rows_own] = 0.5 * paired + LEAKAGE * f * a


def gradient_kernel(means, variances, labels, model, kept, came, gradient):
    m = model[...]
    label = labels[...]
    mean_cell = jnp.zeros(m.shape, F32)
    var_cell = jnp.zeros(m.shape, F32)
    for cluster in range(CLUSTERS):
        mean_cell = jnp.where(label == cluster, means[cluster], mean_cell)
        var_cell = jnp.where(label == cluster, variances[cluster], var_cell)
    gradient[...] = -jnp.exp(m) * (kept[...] + came[...]) + SMALLNESS * (m - mean_cell) / var_cell


def on_device(
    log_conductivity,
    cluster_labels,
    cluster_means,
    cluster_vars,
    source_cells,
    receiver_cells,
    observed,
    warm_potential,
    warm_adjoint,
):
    tile, src = lax.axis_index("tile"), lax.axis_index("src")
    tiles, peers = lax.axis_size("tile"), lax.axis_size("src")
    rows_own, depth, width = log_conductivity.shape
    rows = rows_own * peers
    total_x = width * tiles
    receivers = receiver_cells.shape[0]
    bits = [1 << n for n in range(peers.bit_length() - 1)]
    levels = list(range(len(bits)))
    right = 1 - (tile + src) % 2
    info = jnp.stack([src, right, tile * width]).astype(jnp.int32)
    spots = receiver_cells.T.reshape(1, 2 * receivers)
    spots = jnp.concatenate([spots % total_x, spots // total_x], axis=0)
    spots = jnp.pad(spots, ((0, 6), (0, 0)), constant_values=-1)
    start_v, start_a = warm_potential[0], warm_adjoint[0]

    gathered = log_conductivity[None]
    order = levels[1:] + [0]
    for level in order:
        came = lax.ppermute(gathered, "src", xor_pairs(peers, bits[level]))
        gathered = jnp.concatenate([gathered, came], axis=0)
    other_v = lax.ppermute(start_v, "src", xor_pairs(peers, 1))
    other_a = lax.ppermute(start_a, "src", xor_pairs(peers, 1))
    block = jax.ShapeDtypeStruct((rows // 2, depth, width), F32)
    tile_field = jax.ShapeDtypeStruct((rows, depth, width), F32)
    wide_field = jax.ShapeDtypeStruct((rows, depth, 2 * width), F32)
    payload, model = pl.pallas_call(
        functools.partial(pack_kernel, order),
        out_shape=(block, tile_field),
        in_specs=[SMEM] + [VMEM] * 5,
        out_specs=(VMEM, VMEM),
        compiler_params=PARAMS,
    )(info, gathered, start_v, start_a, other_v, other_a)
    pairs = []
    for t in range(tiles):
        for s in range(peers):
            t_to = (t + 1) % tiles if (t + s) % 2 == 0 else (t - 1) % tiles
            pairs.append((t * peers + s, t_to * peers + s))
    mine = lax.ppermute(payload, ("tile", "src"), pairs)
    theirs = lax.ppermute(mine, "src", xor_pairs(peers, 1))

    field, picked, wide_v, fx, fy, fz, inverse = pl.pallas_call(
        functools.partial(field_kernel, total_x),
        out_shape=(
            jax.ShapeDtypeStruct(warm_potential.shape, F32),
            jax.ShapeDtypeStruct((1, receivers), F32),
        )
        + (wide_field,) * 5,
        in_specs=[SMEM, SMEM] + [VMEM] * 5,
        out_specs=(VMEM,) * 7,
        scratch_shapes=[pltpu.VMEM(wide_field.shape, F32)] * 2,
        compiler_params=PARAMS,
    )(info, source_cells, model, mine, theirs, start_v, spots)

    step = 1
    while step < tiles:
        picked = picked + lax.ppermute(picked, "tile", xor_pairs(tiles, step))
        step *= 2

    places = [0] + levels[:0:-1]
    adjoint, misfit, terms = pl.pallas_call(
        functools.partial(adjoint_kernel, total_x, places),
        out_shape=(
            jax.ShapeDtypeStruct(warm_adjoint.shape, F32),
            jax.ShapeDtypeStruct(observed.shape, F32),
            jax.ShapeDtypeStruct((peers, rows_own, depth, width), F32),
        ),
        in_specs=[SMEM] + [VMEM] * 11,
        out_specs=(VMEM,) * 3,
        scratch_shapes=[pltpu.VMEM(wide_field.shape, F32)] * 3,
        compiler_params=PARAMS,
    )(info, picked, observed, spots, mine, theirs, start_a, wide_v, fx, fy, fz, inverse)

    for level in places[:-1]:
        keep = terms.shape[0] // 2
        terms = terms[:keep] + lax.ppermute(terms[keep:], "src", xor_pairs(peers, bits[level]))
    came = lax.ppermute(terms[1], "src", xor_pairs(peers, bits[places[-1]]))
    gradient = pl.pallas_call(
        gradient_kernel,
        out_shape=jax.ShapeDtypeStruct(log_conductivity.shape, F32),
        in_specs=[SMEM, SMEM] + [VMEM] * 4,
        out_specs=VMEM,
        compiler_params=PARAMS,
    )(cluster_means, cluster_vars, cluster_labels, log_conductivity, terms[0], came)
    return (field, adjoint, misfit, gradient)


def solution(mesh):
    in_specs = (
        P("src", None, "tile"),
        P("src", None, "tile"),
        P(),
        P(),
        P("src", None),
        P(),
        P("src", None),
        P("src", None, None, "tile"),
        P("src", None, None, "tile"),
    )
    out_specs = (
        P("src", None, None, "tile"),
        P("src", None, None, "tile"),
        P("src", None),
        P("src", None, "tile"),
    )
    return jax.shard_map(
        on_device, mesh=mesh, in_specs=in_specs, out_specs=out_specs, check_vma=False
    )
```

```python
import functools

import jax
import jax.numpy as jnp
from jax import lax
from jax.experimental import pallas as pl
from jax.experimental.pallas import tpu as pltpu
from jax.sharding import PartitionSpec as P

SWEEPS = 8
CLUSTERS = 4

LEAKAGE = 0.05
WEIGHT_X = 1.0
WEIGHT_Y = 0.5
WEIGHT_Z = 0.5
SMALLNESS = 1.0

GROUPS = 4
SLOT = 32
HALF = SLOT // 2
PACK_AT = 1
DEPTH = 8

F32 = jnp.float32
BF16 = jnp.bfloat16
VMEM = pl.BlockSpec(memory_space=pltpu.VMEM)
SMEM = pl.BlockSpec(memory_space=pltpu.SMEM)
HBM = pl.BlockSpec(memory_space=pl.ANY)
BESIDE = pl.CostEstimate(flops=0, bytes_accessed=4_000_000, transcendentals=0)
PARAMS = pltpu.CompilerParams(vmem_limit_bytes=24 * 1024 * 1024)


def xor_pairs(count, bit):
    return [(i, i ^ bit) for i in range(count)]


def lane_of(shape):
    return lax.broadcasted_iota(jnp.int32, shape, len(shape) - 1)


def depth_of(shape):
    return lax.broadcasted_iota(jnp.int32, shape, 0)


def turn(values, shift):
    return pltpu.roll(values, shift % 128, 1)


def up_depth(values):
    return pltpu.roll(values, values.shape[0] - 1, 0)


def down_depth(values):
    return pltpu.roll(values, 1, 0)


def full(value, shape):
    return jnp.full(shape, value, jnp.int32)


def each(count, body, unroll):
    def step(k, carry):
        body(k)
        return carry

    lax.fori_loop(0, count, step, 0, unroll=unroll)


def swap_halves(values):
    upper = lane_of(values.shape) % SLOT >= HALF
    return jnp.where(upper, turn(values, HALF), turn(values, -HALF))


def merge(pieces):
    group = lane_of(pieces[0].shape) // SLOT
    out = pieces[0]
    for g in range(1, GROUPS):
        out = jnp.where(group == g, pieces[g], out)
    return out


def rim_columns(shape, width):
    slot = lane_of(shape) % SLOT
    return HALF - 1 - slot + jnp.where(slot < HALF, width, 0)


def edges(row_of, k, per, shape):
    index = (HALF - 1 - lane_of(shape) % SLOT) & 127
    return merge([jnp.take_along_axis(row_of(k + per * g), index, axis=1) for g in range(GROUPS)])


def upper_is(right, shape):
    return (lane_of(shape) % SLOT) // HALF == full(right, shape)


def pack_fields_kernel(info, own_v, own_a, other_v, other_a, passed, payload, passed_on):
    del passed, passed_on
    per = own_v.shape[0] // GROUPS
    shape = own_v.shape[1:]
    mask = upper_is(info[1], shape)

    def body(k):
        for n, (own, other) in enumerate(((own_v, other_v), (own_a, other_a))):
            far = swap_halves(edges(lambda y: other[y], k, per, shape))
            payload[n * per + k] = jnp.where(mask, edges(lambda y: own[y], k, per, shape), far)

    each(per, body, 4)


def pack_model_kernel(order, info, gathered, part, payload, model):
    del part
    peers, rows_own = gathered.shape[:2]
    per = model.shape[0] // GROUPS
    shape = gathered.shape[2:]
    mask = upper_is(info[1], shape)
    for i in range(peers):
        j = sum(((i >> n) & 1) << bit for n, bit in enumerate(order))
        model[pl.ds((info[0] ^ j) * rows_own, rows_own)] = gathered[i]
    for k in range(per // 2):
        first, second = edges(lambda y: model[y], k, per, shape), edges(lambda y: model[y], k + per // 2, per, shape)
        payload[2 * per + k] = jnp.where(mask, first, swap_halves(second))


def own_field_kernel(
    total_x, info, cells, means, variances, labels, own_model, model, warm, observed,
    scale, prior, main, main_2, b_m, b_r, measured, nothing,
):
    rows, depth, width = warm.shape
    shape = (depth, width)
    per = rows // GROUPS
    first_col = info[2]
    nothing[...] = jnp.zeros(nothing.shape, F32)
    measured[...] = jnp.where(full(first_col, observed.shape) == 0, observed[...], 0.0)
    m = own_model[...]
    label = labels[...]
    mean_cell = jnp.zeros(m.shape, F32)
    var_cell = jnp.zeros(m.shape, F32)
    for cluster in range(CLUSTERS):
        mean_cell = jnp.where(label == cluster, means[cluster], mean_cell)
        var_cell = jnp.where(label == cluster, variances[cluster], var_cell)
    scale[...] = -jnp.exp(m)
    prior[...] = SMALLNESS * (m - mean_cell) / var_cell

    def body(k):
        for g in range(GROUPS):
            y = k + per * g
            r = k + (per + 2) * g
            shift = SLOT * g + HALF
            put_row(main, r, turn(warm[y], shift))
            put_row(main_2, r, turn(jnp.exp(model[y]), shift))
            b_m[y] = jnp.zeros(shape, F32)
        b_r[k] = jnp.zeros(shape, F32)

    each(per, body, 2)
    clear_ends(main, per)
    clear_ends(main_2, per)
    lane, depth_at = lane_of(shape), depth_of(shape)
    for n, sign in ((0, 1.0), (1, -1.0)):
        cell = cells[0, n]
        line = cell // total_x
        x = cell - line * total_x
        y = line // depth
        g = y // per
        k = y - g * per
        at_depth = depth_at == line - y * depth
        col_m = first_col + ((lane - (SLOT * g + HALF)) & 127)
        b_m[y] = b_m[y] + jnp.where((col_m == x) & at_depth, sign, 0.0)
        at_slot = (first_col + columns(GROUPS, shape) == x) & (lane // SLOT == g)
        b_r[k] = b_r[k] + jnp.where(at_slot & at_depth, sign, 0.0)


def own_adjoint_kernel(info, mine, theirs, warm, spots, main, rim, hit_x):
    rows, depth, width = warm.shape
    per = rows // GROUPS
    mask = ~upper_is(info[1], (depth, width))

    def body(k):
        for g in range(GROUPS):
            put_row(main, k + (per + 2) * g, turn(warm[k + per * g], SLOT * g + HALF))
        put_row(rim, k, jnp.where(mask, mine[per + k], swap_halves(theirs[per + k])))

    each(per, body, 2)
    clear_ends(main, per)
    at = depth_of((2 * width, spots.shape[1]))
    slot = at % SLOT
    at = info[2] + jnp.where(at < width, at, HALF - 1 - slot + jnp.where(slot < HALF, width, 0))
    hit_x[...] = jnp.where(at == spots[0:1, :], 1.0, 0.0).astype(BF16)


def save_kernel(value, out, sem):
    copy = pltpu.make_async_copy(value, out.at[0], sem)
    copy.start()
    copy.wait()


def at_row(ref, y, shift=0):
    return ref[(y + 1) * DEPTH + shift : (y + 2) * DEPTH + shift, :]


def put_row(ref, y, values):
    start = (y + 1) * DEPTH
    if not isinstance(y, int):
        start = pl.multiple_of(start, DEPTH)
    ref[pl.ds(start, DEPTH), :] = values


def neighbours(main, rim, k, per):
    packed = at_row(rim, k)
    shape = packed.shape
    lane = lane_of(shape)
    slot = lane % SLOT
    own = [at_row(main, g * (per + 2) + k) for g in range(GROUPS)]
    before, after = [], []
    for g in range(GROUPS):
        last = SLOT * g + HALF - 1
        after.append(jnp.where(lane == last, packed, turn(own[g], -1)))
        before.append(jnp.where(lane == last + 1, packed, turn(own[g], 1)))
    inner = merge(own)
    before.append(jnp.where(slot == HALF - 1, inner, turn(packed, -1)))
    after.append(jnp.where(slot == HALF, inner, turn(packed, 1)))
    own.append(packed)
    return own, before, after


def wrap(main, rim, per):
    put_row(rim, -1, turn(at_row(rim, per - 1), SLOT))
    put_row(rim, per, turn(at_row(rim, 0), -SLOT))
    for g in range(1, GROUPS):
        start = g * (per + 2)
        put_row(main, start - 1, turn(at_row(main, start - 3), SLOT))
        put_row(main, start - 2, turn(at_row(main, start), -SLOT))


def clear_ends(main, per):
    put_row(main, -1, jnp.zeros((DEPTH, main.shape[1]), F32))
    put_row(main, GROUPS * (per + 2) - 2, jnp.zeros((DEPTH, main.shape[1]), F32))


def sweep(old, new, face_m, face_r, b_m, b_r):
    per = b_r.shape[0]
    rows = per * GROUPS
    main, rim = old
    main_new, rim_new = new
    for k in range(per):
        own, before, after = neighbours(main, rim, k, per)
        for g in range(GROUPS + 1):
            n = min(g, GROUPS) // GROUPS
            field, face, b = (old[n], (face_m, face_r)[n], (b_m, b_r)[n])
            y = k if n else k + per * g
            r = k if n else k + (per + 2) * g
            c = k if n else k + (per + 1) * g
            total = b[y] + face[0, c + 1] * after[g] + face[1, c + 1] * before[g]
            total = total + (face[3, c + 1] * at_row(field, r, 1) + face[4, c + 1] * at_row(field, r, -1))
            if n or y + 1 < rows:
                total = total + face[2, c + 1] * at_row(field, r + 1)
            if n or y > 0:
                total = total + face[2, c] * at_row(field, r - 1)
            put_row(new[n], r, total * face[5, c + 1])
    wrap(main_new, rim_new, per)


def relax(first, second, face_m, face_r, b_m, b_r):
    per = b_r.shape[0]
    clear_ends(second[0], per)
    wrap(*first, per)

    def two(_, carry):
        sweep(first, second, face_m, face_r, b_m, b_r)
        sweep(second, first, face_m, face_r, b_m, b_r)
        return carry

    lax.fori_loop(0, SWEEPS // 2, two, 0)


def three_parts(values):
    high = values.astype(BF16)
    rest = values - high.astype(F32)
    middle = rest.astype(BF16)
    low = (rest - middle.astype(F32)).astype(BF16)
    return high, middle, low


def columns(g, shape):
    if g == GROUPS:
        return rim_columns(shape, shape[1])
    return (lane_of(shape) - (SLOT * g + HALF)) & 127


def coefficients(total_x, first_col, main, rim, face_m, face_r):
    per = face_r.shape[1] - 1
    rows = per * GROUPS
    shape = face_r.shape[2:]
    group = lane_of(shape) // SLOT
    bottom = depth_of(shape) == shape[0] - 1
    for k in range(per):
        own, before, after = neighbours(main, rim, k, per)
        for g in range(GROUPS + 1):
            n = g // GROUPS
            field, face = ((main, rim)[n], (face_m, face_r)[n])
            y = k if n else k + per * g
            r = k if n else k + (per + 2) * g
            c = k if n else k + (per + 1) * g
            col = first_col + columns(g, shape)
            s = own[g]
            fx = jnp.where((col == total_x - 1) | (col == -1), 0.0, WEIGHT_X * 0.5 * (s + after[g]))
            bx = jnp.where((col == 0) | (col == total_x), 0.0, WEIGHT_X * 0.5 * (before[g] + s))
            fz = jnp.where(bottom, 0.0, WEIGHT_Z * 0.5 * (s + up_depth(s)))
            bz = down_depth(fz)
            fy = WEIGHT_Y * 0.5 * (s + at_row(field, r + 1))
            by = WEIGHT_Y * 0.5 * (at_row(field, r - 1) + s)
            if n and k == 0:
                by = jnp.where(group == 0, 0.0, by)
            if n and k == per - 1:
                fy = jnp.where(group == GROUPS - 1, 0.0, fy)
            if not n and y == 0:
                by = jnp.zeros(shape, F32)
            if not n and y == rows - 1:
                fy = jnp.zeros(shape, F32)
            diagonal = fx + bx + fy + by + fz + bz + LEAKAGE * s
            face[0, c + 1] = fx
            face[1, c + 1] = bx
            face[2, c + 1] = fy
            if not n and k == 0:
                face[2, c] = by
            face[3, c + 1] = fz
            face[4, c + 1] = bz
            face[5, c + 1] = 1.0 / diagonal
    face_r[2, 0] = turn(face_r[2, per], SLOT)


def field_kernel(
    total_x, info, mine, theirs, main_in, sigma_in, b_m, b_r, spots, measured,
    picked, plain, main, rim, face_m, face_r, main_2, rim_2,
):
    del main_in, sigma_in
    rows, depth, width = plain.shape
    shape = (depth, width)
    per = rows // GROUPS
    right, first_col = info[1], info[2]
    mask = ~upper_is(right, shape)
    for k in range(per):
        put_row(rim, k, jnp.where(mask, mine[k], swap_halves(theirs[k])))
    for k in range(per // 2):
        near, far = mine[2 * per + k], theirs[2 * per + k]
        put_row(rim_2, k, jnp.exp(jnp.where(mask, near, far)))
        put_row(rim_2, k + per // 2, jnp.exp(swap_halves(jnp.where(mask, far, near))))
    wrap(main_2, rim_2, per)
    coefficients(total_x, first_col, main_2, rim_2, face_m, face_r)
    relax((main, rim), (main_2, rim_2), face_m, face_r, b_m, b_r)
    for y in range(rows):
        plain[y] = turn(at_row(main, y + 2 * (y // per)), -(SLOT * (y // per) + HALF))
    count = spots.shape[1]
    x_row = spots[0:1, :] - first_col
    line_row = spots[1:2, :]
    hit_x = jnp.where(depth_of((width, count)) == x_row, 1.0, 0.0).astype(BF16)
    flat = plain[...].reshape(rows * depth, width)
    lines = sum(jnp.dot(part, hit_x, preferred_element_type=F32) for part in three_parts(flat))
    hit_line = depth_of((rows * depth, count)) == line_row
    got = jnp.sum(jnp.where(hit_line, lines, 0.0), axis=0, keepdims=True)
    picked[...] = got[:, : count // 2] - got[:, count // 2 :] - measured[...]


def adjoint_kernel(
    total_x, places, info, picked, spots, main_in, rim_in, hit_x, main_v, rim_v, face_m, face_r,
    misfit_out, terms, plain, main, rim, main_2, rim_2, b_m, b_r,
):
    del main_in, rim_in
    rows, depth, width = plain.shape
    shape = (depth, width)
    per = rows // GROUPS
    me, first_col = info[0], info[2]
    count = spots.shape[1]
    misfit = picked[...]
    misfit_out[...] = misfit
    weights = jnp.concatenate([misfit, -misfit], axis=1)
    hit_line = depth_of((rows * depth, count)) == spots[1:2, :]
    flat = jnp.zeros((rows * depth, 2 * width), F32)
    for part in three_parts(weights):
        left = jnp.where(hit_line, part.astype(F32), 0.0).astype(BF16)
        flat = flat + lax.dot_general(left, hit_x[...], (((1,), (1,)), ((), ())), preferred_element_type=F32)
    flat = flat.reshape(rows, depth, 2 * width)
    for y in range(rows):
        b_m[y] = turn(flat[y, :, :width], SLOT * (y // per) + HALF)
    for k in range(per):
        b_r[k] = merge([flat[k + per * g, :, width:] for g in range(GROUPS)])
    relax((main, rim), (main_2, rim_2), face_m, face_r, b_m, b_r)
    for y in range(rows):
        plain[y] = turn(at_row(main, y + 2 * (y // per)), -(SLOT * (y // per) + HALF))
    rows_own = terms.shape[1]
    bottom = depth_of(shape) == depth - 1
    for k in range(per):
        f_own, f_before, f_after = neighbours(main_v, rim_v, k, per)
        a_own, a_before, a_after = neighbours(main, rim, k, per)
        for g in range(GROUPS):
            y, r = k + per * g, k + (per + 2) * g
            col = first_col + columns(g, shape)
            f, a = f_own[g], a_own[g]
            px_next = jnp.where(col == total_x - 1, 0.0, (f_after[g] - f) * (a_after[g] - a))
            px_prev = jnp.where(col == 0, 0.0, (f - f_before[g]) * (a - a_before[g]))
            py = jnp.zeros(shape, F32)
            if y + 1 < rows:
                py = py + (at_row(main_v, r + 1) - f) * (at_row(main, r + 1) - a)
            if y > 0:
                py = py + (f - at_row(main_v, r - 1)) * (a - at_row(main, r - 1))
            pz = jnp.where(bottom, 0.0, (at_row(main_v, r, 1) - f) * (at_row(main, r, 1) - a))
            pz = pz + down_depth(pz)
            paired = WEIGHT_X * (px_prev + px_next) + WEIGHT_Y * py + WEIGHT_Z * pz
            j = me ^ (y // rows_own)
            place = sum(((j >> bit) & 1) << n for n, bit in enumerate(reversed(places)))
            term = 0.5 * paired + LEAKAGE * f * a
            terms[place, y % rows_own] = turn(term, -(SLOT * g + HALF))


def gradient_kernel(scale, prior, kept, came, gradient):
    gradient[...] = scale[...] * (kept[...] + came[...]) + prior[...]


def on_device(
    log_conductivity,
    cluster_labels,
    cluster_means,
    cluster_vars,
    source_cells,
    receiver_cells,
    observed,
    warm_potential,
    warm_adjoint,
):
    tile, src = lax.axis_index("tile"), lax.axis_index("src")
    tiles, peers = lax.axis_size("tile"), lax.axis_size("src")
    rows_own, depth, width = log_conductivity.shape
    rows = rows_own * peers
    per = rows // GROUPS
    total_x = width * tiles
    receivers = receiver_cells.shape[0]
    bits = [1 << n for n in range(peers.bit_length() - 1)]
    levels = list(range(len(bits)))
    right = 1 - (tile + src) % 2
    info = jnp.stack([src, right, tile * width]).astype(jnp.int32)
    spots = receiver_cells.T.reshape(1, 2 * receivers)
    spots = jnp.concatenate([spots % total_x, spots // total_x], axis=0)
    spots = jnp.pad(spots, ((0, 6), (0, 0)), constant_values=-1)
    start_v, start_a = warm_potential[0], warm_adjoint[0]

    def shaped(*sizes):
        return jax.ShapeDtypeStruct(sizes, F32)

    other_v = lax.ppermute(start_v, "src", xor_pairs(peers, 1))
    other_a = lax.ppermute(start_a, "src", xor_pairs(peers, 1))
    order = levels[:0:-1] + [0]
    own = log_conductivity[None]
    gathered = lax.optimization_barrier(jnp.pad(own, ((0, peers - 1), (0, 0), (0, 0), (0, 0))))
    for n, level in enumerate(order):
        sent = own if n == 0 else gathered[: 1 << n]
        came = lax.ppermute(sent, "src", xor_pairs(peers, bits[level]))
        if n == PACK_AT:
            payload, gathered = pl.pallas_call(
                pack_fields_kernel,
                out_shape=(shaped(5 * per // 2, depth, width), shaped(*gathered.shape)),
                in_specs=[SMEM] + [VMEM] * 5,
                out_specs=(VMEM, VMEM),
                input_output_aliases={5: 1},
                cost_estimate=BESIDE,
                compiler_params=PARAMS,
            )(info, start_v, start_a, other_v, other_a, gathered)
        gathered = lax.dynamic_update_slice(gathered, came, (1 << n, 0, 0, 0))
    payload, model = pl.pallas_call(
        functools.partial(pack_model_kernel, order),
        out_shape=(shaped(*payload.shape), shaped(rows, depth, width)),
        in_specs=[SMEM, VMEM, VMEM],
        out_specs=(VMEM, VMEM),
        input_output_aliases={2: 0},
        compiler_params=PARAMS,
    )(info, gathered, payload)
    pairs = []
    for t in range(tiles):
        for s in range(peers):
            t_to = (t + 1) % tiles if (t + s) % 2 == 0 else (t - 1) % tiles
            pairs.append((t * peers + s, t_to * peers + s))
    mine = lax.ppermute(payload, ("tile", "src"), pairs)
    main_shape, rim_shape = ((rows + 2 * GROUPS) * depth, width), ((per + 2) * depth, width)
    scale, prior, main_v, sigma, b_m, b_r, measured, nothing = pl.pallas_call(
        functools.partial(own_field_kernel, total_x),
        out_shape=(shaped(*log_conductivity.shape),) * 2
        + (shaped(*main_shape),) * 2
        + (
            shaped(rows, depth, width),
            shaped(per, depth, width),
            shaped(*observed.shape),
            shaped(1, depth, width),
        ),
        in_specs=[SMEM] * 4 + [VMEM] * 5,
        out_specs=(VMEM,) * 8,
        cost_estimate=BESIDE,
        compiler_params=PARAMS,
    )(
        info, source_cells, cluster_means, cluster_vars, cluster_labels, log_conductivity,
        model, start_v, observed,
    )
    theirs = lax.ppermute(mine + nothing, "src", xor_pairs(peers, 1))
    picked, plain_v, main_v, rim_v, face_m, face_r, _ = pl.pallas_call(
        functools.partial(field_kernel, total_x),
        out_shape=(
            shaped(1, receivers),
            shaped(rows, depth, width),
            shaped(*main_shape),
            shaped(*rim_shape),
            shaped(6, rows + GROUPS, depth, width),
            shaped(6, per + 1, depth, width),
            shaped(*main_shape),
        ),
        in_specs=[SMEM] + [VMEM] * 8,
        out_specs=(VMEM,) * 7,
        input_output_aliases={3: 2, 4: 6},
        scratch_shapes=[pltpu.VMEM(rim_shape, F32)],
        compiler_params=PARAMS,
    )(info, mine, theirs, main_v, sigma, b_m, b_r, spots, measured)
    main_a, rim_a, hit_x = pl.pallas_call(
        own_adjoint_kernel,
        out_shape=(
            shaped(*main_shape),
            shaped(*rim_shape),
            jax.ShapeDtypeStruct((2 * width, 2 * receivers), BF16),
        ),
        in_specs=[SMEM] + [VMEM] * 4,
        out_specs=(VMEM,) * 3,
        cost_estimate=BESIDE,
        compiler_params=PARAMS,
    )(info, mine, theirs, start_a, spots)

    def saved(value, shape):
        return pl.pallas_call(
            save_kernel,
            out_shape=shaped(*shape),
            in_specs=[VMEM],
            out_specs=HBM,
            scratch_shapes=[pltpu.SemaphoreType.DMA],
            cost_estimate=BESIDE,
            compiler_params=PARAMS,
        )(value)

    field = saved(plain_v, warm_potential.shape)
    step = 1
    while step < tiles:
        picked = picked + lax.ppermute(picked, "tile", xor_pairs(tiles, step))
        step *= 2

    misfit, terms, plain_a, _, _ = pl.pallas_call(
        functools.partial(adjoint_kernel, total_x, levels),
        out_shape=(
            shaped(*observed.shape),
            shaped(peers, rows_own, depth, width),
            shaped(rows, depth, width),
            shaped(*main_shape),
            shaped(*rim_shape),
        ),
        in_specs=[SMEM] + [VMEM] * 9,
        out_specs=(VMEM,) * 5,
        input_output_aliases={3: 3, 4: 4},
        scratch_shapes=[
            pltpu.VMEM(main_shape, F32),
            pltpu.VMEM(rim_shape, F32),
            pltpu.VMEM((rows, depth, width), F32),
            pltpu.VMEM((per, depth, width), F32),
        ],
        compiler_params=PARAMS,
    )(info, picked, spots, main_a, rim_a, hit_x, main_v, rim_v, face_m, face_r)
    adjoint = saved(plain_a, warm_adjoint.shape)

    for level in levels[:-1]:
        keep = terms.shape[0] // 2
        terms = terms[:keep] + lax.ppermute(terms[keep:], "src", xor_pairs(peers, bits[level]))
    came = lax.ppermute(terms[1], "src", xor_pairs(peers, bits[-1]))
    gradient = pl.pallas_call(
        gradient_kernel,
        out_shape=shaped(*log_conductivity.shape),
        in_specs=[VMEM] * 4,
        out_specs=VMEM,
        compiler_params=PARAMS,
    )(scale, prior, terms[0], came)
    return (field, adjoint, misfit, gradient)


def solution(mesh):
    in_specs = (
        P("src", None, "tile"),
        P("src", None, "tile"),
        P(),
        P(),
        P("src", None),
        P(),
        P("src", None),
        P("src", None, None, "tile"),
        P("src", None, None, "tile"),
    )
    out_specs = (
        P("src", None, None, "tile"),
        P("src", None, None, "tile"),
        P("src", None),
        P("src", None, "tile"),
    )
    return jax.shard_map(
        on_device, mesh=mesh, in_specs=in_specs, out_specs=out_specs, check_vma=False
    )
```

```python
import functools

import jax
import jax.numpy as jnp
from jax import lax
from jax.experimental import pallas as pl
from jax.experimental.pallas import tpu as pltpu
from jax.sharding import PartitionSpec as P

SWEEPS = 8
CLUSTERS = 4

LEAKAGE = 0.05
WEIGHT_X = 1.0
WEIGHT_Y = 0.5
WEIGHT_Z = 0.5
SMALLNESS = 1.0

GROUPS = 4
EDGE = SWEEPS + 1
SLOT = 32
HALF = SLOT // 2
PACK_AT = 1
DEPTH = 8

F32 = jnp.float32
BF16 = jnp.bfloat16
VMEM = pl.BlockSpec(memory_space=pltpu.VMEM)
SMEM = pl.BlockSpec(memory_space=pltpu.SMEM)
HBM = pl.BlockSpec(memory_space=pl.ANY)
BESIDE = pl.CostEstimate(flops=0, bytes_accessed=4_000_000, transcendentals=0)
PARAMS = pltpu.CompilerParams(vmem_limit_bytes=24 * 1024 * 1024)


def facing():
    return 1 - (lax.axis_index("tile") + lax.axis_index("src")) % 2


def xor_pairs(count, bit):
    return [(i, i ^ bit) for i in range(count)]


def lane_of(shape):
    return lax.broadcasted_iota(jnp.int32, shape, len(shape) - 1)


def depth_of(shape):
    return lax.broadcasted_iota(jnp.int32, shape, 0)


def turn(values, shift):
    return pltpu.roll(values, shift % 128, 1)


def up_depth(values):
    return pltpu.roll(values, values.shape[0] - 1, 0)


def down_depth(values):
    return pltpu.roll(values, 1, 0)


def full(value, shape):
    return jnp.full(shape, value, jnp.int32)


def each(count, body, unroll):
    def step(k, carry):
        body(k)
        return carry

    lax.fori_loop(0, count, step, 0, unroll=unroll)


def window(side, offset, shape):
    slot = ((lane_of(shape) - offset) & 127) % SLOT
    low = full(HALF - EDGE + EDGE * side, shape)
    return (slot >= low) & (slot < low + EDGE)


def joined(side, first, second, third):
    shape = first.shape
    out = jnp.where(window(side, 0, shape), first, turn(second, EDGE))
    return jnp.where(window(side, -EDGE, shape), turn(third, -EDGE), out)


def merge(pieces):
    group = lane_of(pieces[0].shape) // SLOT
    out = pieces[0]
    for g in range(1, GROUPS):
        out = jnp.where(group == g, pieces[g], out)
    return out


def rim_columns(shape, width):
    slot = lane_of(shape) % SLOT
    return HALF - 1 - slot + jnp.where(slot < HALF, width, 0)


def edges(row_of, k, per, shape):
    index = (HALF - 1 - lane_of(shape) % SLOT) & 127
    return merge([jnp.take_along_axis(row_of(k + per * g), index, axis=1) for g in range(GROUPS)])


def message_rows(per):
    return per + per // 2 + -(-(per // 2) // 3)


def model_place(k, per):
    if k < per // 2:
        return per + k, -EDGE
    k -= per // 2
    return per + per // 2 + k // 3, (0, EDGE, -EDGE)[k % 3]


def pack_fields_kernel(own_v, own_a, other_v, other_a, passed, payload, passed_on):
    del passed, passed_on
    per = own_v.shape[0] // GROUPS
    shape = own_v.shape[1:]
    side = facing()

    def part(ref, k):
        return edges(lambda y: ref[y], k, per, shape)

    def body(h):
        for k in (2 * h, 2 * h + 1):
            payload[k] = joined(side, part(own_v, k), part(other_v, k), part(own_a, k))
        first, second = part(other_a, 2 * h), part(other_a, 2 * h + 1)
        payload[per + h] = jnp.where(window(side, 0, shape), first, turn(second, EDGE))

    each(per // 2, body, 2)


def pack_model_kernel(order, gathered, part, payload, model):
    peers, rows_own = gathered.shape[:2]
    per = model.shape[0] // GROUPS
    shape = gathered.shape[2:]
    side = facing()
    for i in range(peers):
        j = sum(((i >> n) & 1) << bit for n, bit in enumerate(order))
        model[pl.ds((lax.axis_index("src") ^ j) * rows_own, rows_own)] = gathered[i]
    packed = [edges(lambda y: model[y], k, per, shape) for k in range(per)]
    half = per // 2
    for h in range(half):
        payload[per + h] = jnp.where(window(side, -EDGE, shape), turn(packed[h], -EDGE), part[per + h])
    for n, k in enumerate(range(half, per, 3)):
        payload[per + half + n] = joined(side, *[packed[min(k + m, per - 1)] for m in range(3)])


def own_field_kernel(
    total_x, cells, means, variances, labels, own_model, model, warm, observed,
    scale, prior, main, main_2, b_m, b_r, measured, nothing,
):
    rows, depth, width = warm.shape
    shape = (depth, width)
    per = rows // GROUPS
    first_col = lax.axis_index("tile") * width
    nothing[...] = jnp.zeros(nothing.shape, F32)
    measured[...] = jnp.where(full(first_col, observed.shape) == 0, observed[...], 0.0)
    m = own_model[...]
    label = labels[...]
    mean_cell = jnp.zeros(m.shape, F32)
    var_cell = jnp.zeros(m.shape, F32)
    for cluster in range(CLUSTERS):
        mean_cell = jnp.where(label == cluster, means[cluster], mean_cell)
        var_cell = jnp.where(label == cluster, variances[cluster], var_cell)
    scale[...] = -jnp.exp(m)
    prior[...] = SMALLNESS * (m - mean_cell) / var_cell

    def body(k):
        for g in range(GROUPS):
            y = k + per * g
            r = k + (per + 2) * g
            shift = SLOT * g + HALF
            put_row(main, r, turn(warm[y], shift))
            put_row(main_2, r, turn(jnp.exp(model[y]), shift))
            b_m[y] = jnp.zeros(shape, F32)
        b_r[k] = jnp.zeros(shape, F32)

    each(per, body, 2)
    clear_ends(main, per)
    clear_ends(main_2, per)
    lane, depth_at = lane_of(shape), depth_of(shape)
    for n, sign in ((0, 1.0), (1, -1.0)):
        cell = cells[0, n]
        line = cell // total_x
        x = cell - line * total_x
        y = line // depth
        g = y // per
        k = y - g * per
        at_depth = depth_at == line - y * depth
        col_m = first_col + ((lane - (SLOT * g + HALF)) & 127)
        b_m[y] = b_m[y] + jnp.where((col_m == x) & at_depth, sign, 0.0)
        at_slot = (first_col + columns(GROUPS, shape) == x) & (lane // SLOT == g)
        b_r[k] = b_r[k] + jnp.where(at_slot & at_depth, sign, 0.0)


def own_adjoint_kernel(mine, theirs, warm, spots, main, rim, hit_x):
    rows, depth, width = warm.shape
    per = rows // GROUPS
    mask = window(1 - facing(), 0, (depth, width))

    def body(h):
        for n in range(2):
            k = 2 * h + n
            for g in range(GROUPS):
                put_row(main, k + (per + 2) * g, turn(warm[k + per * g], SLOT * g + HALF))
            far = turn(theirs[per + h], -EDGE * n)
            put_row(rim, k, jnp.where(mask, turn(mine[k], EDGE), far))

    each(per // 2, body, 1)
    clear_ends(main, per)
    at = depth_of((2 * width, spots.shape[1]))
    slot = at % SLOT
    at = lax.axis_index("tile") * width + jnp.where(at < width, at, HALF - 1 - slot + jnp.where(slot < HALF, width, 0))
    hit_x[...] = jnp.where(at == spots[0:1, :], 1.0, 0.0).astype(BF16)


def save_kernel(field, adjoint, misfit, field_out, adjoint_out, misfit_out, sems):
    pairs = ((field, field_out.at[0]), (adjoint, adjoint_out.at[0]), (misfit, misfit_out))
    copies = [pltpu.make_async_copy(a, b, sems.at[n]) for n, (a, b) in enumerate(pairs)]
    for copy in copies:
        copy.start()
    for copy in copies:
        copy.wait()


def at_row(ref, y, shift=0):
    return ref[(y + 1) * DEPTH + shift : (y + 2) * DEPTH + shift, :]


def put_row(ref, y, values):
    start = (y + 1) * DEPTH
    if not isinstance(y, int):
        start = pl.multiple_of(start, DEPTH)
    ref[pl.ds(start, DEPTH), :] = values


def row_set(main, rim, k, per):
    return [at_row(main, g * (per + 2) + k) for g in range(GROUPS)] + [at_row(rim, k)]


def beside(own):
    packed = own[GROUPS]
    lane = lane_of(packed.shape)
    slot = lane % SLOT
    before, after = [], []
    for g in range(GROUPS):
        last = SLOT * g + HALF - 1
        after.append(jnp.where(lane == last, packed, turn(own[g], -1)))
        before.append(jnp.where(lane == last + 1, packed, turn(own[g], 1)))
    inner = merge(own[:GROUPS])
    before.append(jnp.where(slot == HALF - 1, inner, turn(packed, -1)))
    after.append(jnp.where(slot == HALF, inner, turn(packed, 1)))
    return before, after


def wrap(main, rim, per):
    put_row(rim, -1, turn(at_row(rim, per - 1), SLOT))
    put_row(rim, per, turn(at_row(rim, 0), -SLOT))
    for g in range(1, GROUPS):
        start = g * (per + 2)
        put_row(main, start - 1, turn(at_row(main, start - 3), SLOT))
        put_row(main, start - 2, turn(at_row(main, start), -SLOT))


def clear_ends(main, per):
    put_row(main, -1, jnp.zeros((DEPTH, main.shape[1]), F32))
    put_row(main, GROUPS * (per + 2) - 2, jnp.zeros((DEPTH, main.shape[1]), F32))


def sweep(old, new, face_m, face_r, b_m, b_r):
    per = b_r.shape[0]
    main_new, rim_new = new
    above, own = row_set(*old, -1, per), row_set(*old, 0, per)
    face_above = [face_m[2, (per + 1) * g] for g in range(GROUPS)] + [face_r[2, 0]]
    for k in range(per):
        below = row_set(*old, k + 1, per)
        before, after = beside(own)
        for g in range(GROUPS + 1):
            n = g // GROUPS
            field, face, b = (old[n], (face_m, face_r)[n], (b_m, b_r)[n])
            y = k if n else k + per * g
            r = k if n else k + (per + 2) * g
            c = k if n else k + (per + 1) * g
            fy, fz = face[2, c + 1], face[3, c + 1]
            total = b[y] + face[0, c + 1] * after[g] + face[1, c + 1] * before[g]
            total = total + (fz * up_depth(own[g]) + down_depth(fz * own[g]))
            total = total + (fy * below[g] + face_above[g] * above[g])
            face_above[g] = fy
            put_row(new[n], r, total * face[5, c + 1])
        above, own = own, below
    wrap(main_new, rim_new, per)


def relax(first, second, face_m, face_r, b_m, b_r):
    per = b_r.shape[0]
    clear_ends(second[0], per)
    wrap(*first, per)

    def two(_, carry):
        sweep(first, second, face_m, face_r, b_m, b_r)
        sweep(second, first, face_m, face_r, b_m, b_r)
        return carry

    lax.fori_loop(0, SWEEPS // 2, two, 0)


def three_parts(values):
    high = values.astype(BF16)
    rest = values - high.astype(F32)
    middle = rest.astype(BF16)
    low = (rest - middle.astype(F32)).astype(BF16)
    return high, middle, low


def columns(g, shape):
    if g == GROUPS:
        return rim_columns(shape, shape[1])
    return (lane_of(shape) - (SLOT * g + HALF)) & 127


def coefficients(total_x, first_col, main, rim, face_m, face_r):
    per = face_r.shape[1] - 1
    rows = per * GROUPS
    shape = face_r.shape[2:]
    group = lane_of(shape) // SLOT
    bottom = depth_of(shape) == shape[0] - 1
    for k in range(per):
        own = row_set(main, rim, k, per)
        before, after = beside(own)
        for g in range(GROUPS + 1):
            n = g // GROUPS
            field, face = ((main, rim)[n], (face_m, face_r)[n])
            y = k if n else k + per * g
            r = k if n else k + (per + 2) * g
            c = k if n else k + (per + 1) * g
            col = first_col + columns(g, shape)
            s = own[g]
            fx = jnp.where((col == total_x - 1) | (col == -1), 0.0, WEIGHT_X * 0.5 * (s + after[g]))
            bx = jnp.where((col == 0) | (col == total_x), 0.0, WEIGHT_X * 0.5 * (before[g] + s))
            fz = jnp.where(bottom, 0.0, WEIGHT_Z * 0.5 * (s + up_depth(s)))
            bz = down_depth(fz)
            fy = WEIGHT_Y * 0.5 * (s + at_row(field, r + 1))
            by = WEIGHT_Y * 0.5 * (at_row(field, r - 1) + s)
            if n and k == 0:
                by = jnp.where(group == 0, 0.0, by)
            if n and k == per - 1:
                fy = jnp.where(group == GROUPS - 1, 0.0, fy)
            if not n and y == 0:
                by = jnp.zeros(shape, F32)
            if not n and y == rows - 1:
                fy = jnp.zeros(shape, F32)
            diagonal = fx + bx + fy + by + fz + bz + LEAKAGE * s
            face[0, c + 1] = fx
            face[1, c + 1] = bx
            face[2, c + 1] = fy
            if not n and k == 0:
                face[2, c] = by
            face[3, c + 1] = fz
            face[4, c + 1] = bz
            face[5, c + 1] = 1.0 / diagonal
    face_r[2, 0] = turn(face_r[2, per], SLOT)


def field_kernel(
    total_x, mine, theirs, main_in, sigma_in, b_m, b_r, spots, measured,
    picked, plain, main, rim, face_m, face_r, main_2, rim_2,
):
    del main_in, sigma_in
    rows, depth, width = plain.shape
    shape = (depth, width)
    per = rows // GROUPS
    first_col = lax.axis_index("tile") * width
    mask = window(1 - facing(), 0, shape)
    filled = mask | window(facing(), 0, shape)
    for k in range(per):
        put_row(rim, k, jnp.where(mask, mine[k], turn(theirs[k], -EDGE)))
        row, offset = model_place(k, per)
        beyond = turn(jnp.where(window(1 - facing(), offset, shape), mine[row], theirs[row]), -offset)
        put_row(rim_2, k, jnp.exp(jnp.where(filled, beyond, 0.0)))
    wrap(main_2, rim_2, per)
    coefficients(total_x, first_col, main_2, rim_2, face_m, face_r)
    relax((main, rim), (main_2, rim_2), face_m, face_r, b_m, b_r)
    for y in range(rows):
        plain[y] = turn(at_row(main, y + 2 * (y // per)), -(SLOT * (y // per) + HALF))
    count = spots.shape[1]
    x_row = spots[0:1, :] - first_col
    line_row = spots[1:2, :]
    hit_x = jnp.where(depth_of((width, count)) == x_row, 1.0, 0.0).astype(BF16)
    flat = plain[...].reshape(rows * depth, width)
    lines = sum(jnp.dot(part, hit_x, preferred_element_type=F32) for part in three_parts(flat))
    hit_line = depth_of((rows * depth, count)) == line_row
    got = jnp.sum(jnp.where(hit_line, lines, 0.0), axis=0, keepdims=True)
    picked[...] = got[:, : count // 2] - got[:, count // 2 :] - measured[...]


def adjoint_kernel(
    total_x, places, picked, spots, main_in, rim_in, hit_x, main_v, rim_v, face_m, face_r,
    terms, plain, main, rim, main_2, rim_2, b_m, b_r,
):
    del main_in, rim_in
    rows, depth, width = plain.shape
    shape = (depth, width)
    per = rows // GROUPS
    me = lax.axis_index("src")
    first_col = lax.axis_index("tile") * width
    count = spots.shape[1]
    misfit = picked[...]
    weights = jnp.concatenate([misfit, -misfit], axis=1)
    hit_line = depth_of((rows * depth, count)) == spots[1:2, :]
    flat = jnp.zeros((rows * depth, 2 * width), F32)
    for part in three_parts(weights):
        left = jnp.where(hit_line, part.astype(F32), 0.0).astype(BF16)
        flat = flat + lax.dot_general(left, hit_x[...], (((1,), (1,)), ((), ())), preferred_element_type=F32)
    flat = flat.reshape(rows, depth, 2 * width)
    for y in range(rows):
        b_m[y] = turn(flat[y, :, :width], SLOT * (y // per) + HALF)
    for k in range(per):
        b_r[k] = merge([flat[k + per * g, :, width:] for g in range(GROUPS)])
    relax((main, rim), (main_2, rim_2), face_m, face_r, b_m, b_r)
    for y in range(rows):
        plain[y] = turn(at_row(main, y + 2 * (y // per)), -(SLOT * (y // per) + HALF))
    rows_own = terms.shape[1]
    bottom = depth_of(shape) == depth - 1
    for k in range(per):
        f_own, a_own = row_set(main_v, rim_v, k, per), row_set(main, rim, k, per)
        f_before, f_after = beside(f_own)
        a_before, a_after = beside(a_own)
        for g in range(GROUPS):
            y, r = k + per * g, k + (per + 2) * g
            col = first_col + columns(g, shape)
            f, a = f_own[g], a_own[g]
            px_next = jnp.where(col == total_x - 1, 0.0, (f_after[g] - f) * (a_after[g] - a))
            px_prev = jnp.where(col == 0, 0.0, (f - f_before[g]) * (a - a_before[g]))
            py = jnp.zeros(shape, F32)
            if y + 1 < rows:
                py = py + (at_row(main_v, r + 1) - f) * (at_row(main, r + 1) - a)
            if y > 0:
                py = py + (f - at_row(main_v, r - 1)) * (a - at_row(main, r - 1))
            pz = jnp.where(bottom, 0.0, (at_row(main_v, r, 1) - f) * (at_row(main, r, 1) - a))
            pz = pz + down_depth(pz)
            paired = WEIGHT_X * (px_prev + px_next) + WEIGHT_Y * py + WEIGHT_Z * pz
            j = me ^ (y // rows_own)
            place = sum(((j >> bit) & 1) << n for n, bit in enumerate(reversed(places)))
            term = 0.5 * paired + LEAKAGE * f * a
            terms[place, y % rows_own] = turn(term, -(SLOT * g + HALF))


def gradient_kernel(scale, prior, kept, came, gradient):
    gradient[...] = scale[...] * (kept[...] + came[...]) + prior[...]


def on_device(
    log_conductivity,
    cluster_labels,
    cluster_means,
    cluster_vars,
    source_cells,
    receiver_cells,
    observed,
    warm_potential,
    warm_adjoint,
):
    tile, src = lax.axis_index("tile"), lax.axis_index("src")
    tiles, peers = lax.axis_size("tile"), lax.axis_size("src")
    rows_own, depth, width = log_conductivity.shape
    rows = rows_own * peers
    per = rows // GROUPS
    total_x = width * tiles
    receivers = receiver_cells.shape[0]
    bits = [1 << n for n in range(peers.bit_length() - 1)]
    levels = list(range(len(bits)))
    spots = receiver_cells.T.reshape(1, 2 * receivers)
    spots = jnp.concatenate([spots % total_x, spots // total_x], axis=0)
    spots = jnp.pad(spots, ((0, 6), (0, 0)), constant_values=-1)
    start_v, start_a = warm_potential[0], warm_adjoint[0]

    def shaped(*sizes):
        return jax.ShapeDtypeStruct(sizes, F32)

    other_v = lax.ppermute(start_v, "src", xor_pairs(peers, 1))
    other_a = lax.ppermute(start_a, "src", xor_pairs(peers, 1))
    order = levels[:0:-1] + [0]
    own = log_conductivity[None]
    gathered = lax.optimization_barrier(jnp.pad(own, ((0, peers - 1), (0, 0), (0, 0), (0, 0))))
    for n, level in enumerate(order):
        sent = own if n == 0 else gathered[: 1 << n]
        came = lax.ppermute(sent, "src", xor_pairs(peers, bits[level]))
        if n == PACK_AT:
            payload, gathered = pl.pallas_call(
                pack_fields_kernel,
                out_shape=(shaped(message_rows(per), depth, width), shaped(*gathered.shape)),
                in_specs=[VMEM] * 5,
                out_specs=(VMEM, VMEM),
                input_output_aliases={4: 1},
                cost_estimate=BESIDE,
                compiler_params=PARAMS,
            )(start_v, start_a, other_v, other_a, gathered)
        gathered = lax.dynamic_update_slice(gathered, came, (1 << n, 0, 0, 0))
    payload, model = pl.pallas_call(
        functools.partial(pack_model_kernel, order),
        out_shape=(shaped(*payload.shape), shaped(rows, depth, width)),
        in_specs=[VMEM, VMEM],
        out_specs=(VMEM, VMEM),
        input_output_aliases={1: 0},
        compiler_params=PARAMS,
    )(gathered, payload)
    pairs = []
    for t in range(tiles):
        for s in range(peers):
            t_to = (t + 1) % tiles if (t + s) % 2 == 0 else (t - 1) % tiles
            pairs.append((t * peers + s, t_to * peers + s))
    mine = lax.ppermute(payload, ("tile", "src"), pairs)
    main_shape, rim_shape = ((rows + 2 * GROUPS) * depth, width), ((per + 2) * depth, width)
    scale, prior, main_v, sigma, b_m, b_r, measured, nothing = pl.pallas_call(
        functools.partial(own_field_kernel, total_x),
        out_shape=(shaped(*log_conductivity.shape),) * 2
        + (shaped(*main_shape),) * 2
        + (
            shaped(rows, depth, width),
            shaped(per, depth, width),
            shaped(*observed.shape),
            shaped(1, depth, width),
        ),
        in_specs=[SMEM] * 3 + [VMEM] * 5,
        out_specs=(VMEM,) * 8,
        cost_estimate=BESIDE,
        compiler_params=PARAMS,
    )(
        source_cells, cluster_means, cluster_vars, cluster_labels, log_conductivity,
        model, start_v, observed,
    )
    theirs = lax.ppermute(mine + nothing, "src", xor_pairs(peers, 1))
    picked, plain_v, main_v, rim_v, face_m, face_r, _ = pl.pallas_call(
        functools.partial(field_kernel, total_x),
        out_shape=(
            shaped(1, receivers),
            shaped(rows, depth, width),
            shaped(*main_shape),
            shaped(*rim_shape),
            shaped(6, rows + GROUPS, depth, width),
            shaped(6, per + 1, depth, width),
            shaped(*main_shape),
        ),
        in_specs=[VMEM] * 8,
        out_specs=(VMEM,) * 7,
        input_output_aliases={2: 2, 3: 6},
        scratch_shapes=[pltpu.VMEM(rim_shape, F32)],
        compiler_params=PARAMS,
    )(mine, theirs, main_v, sigma, b_m, b_r, spots, measured)
    main_a, rim_a, hit_x = pl.pallas_call(
        own_adjoint_kernel,
        out_shape=(
            shaped(*main_shape),
            shaped(*rim_shape),
            jax.ShapeDtypeStruct((2 * width, 2 * receivers), BF16),
        ),
        in_specs=[VMEM] * 4,
        out_specs=(VMEM,) * 3,
        cost_estimate=BESIDE,
        compiler_params=PARAMS,
    )(mine, theirs, start_a, spots)

    step = 1
    while step < tiles:
        picked = picked + lax.ppermute(picked, "tile", xor_pairs(tiles, step))
        step *= 2

    terms, plain_a, _, _ = pl.pallas_call(
        functools.partial(adjoint_kernel, total_x, levels),
        out_shape=(
            shaped(peers, rows_own, depth, width),
            shaped(rows, depth, width),
            shaped(*main_shape),
            shaped(*rim_shape),
        ),
        in_specs=[VMEM] * 9,
        out_specs=(VMEM,) * 4,
        input_output_aliases={2: 2, 3: 3},
        scratch_shapes=[
            pltpu.VMEM(main_shape, F32),
            pltpu.VMEM(rim_shape, F32),
            pltpu.VMEM((rows, depth, width), F32),
            pltpu.VMEM((per, depth, width), F32),
        ],
        compiler_params=PARAMS,
    )(picked, spots, main_a, rim_a, hit_x, main_v, rim_v, face_m, face_r)
    field, adjoint, misfit = pl.pallas_call(
        save_kernel,
        out_shape=(shaped(*warm_potential.shape), shaped(*warm_adjoint.shape), shaped(*observed.shape)),
        in_specs=[VMEM] * 3,
        out_specs=(HBM,) * 3,
        scratch_shapes=[pltpu.SemaphoreType.DMA((3,))],
        cost_estimate=BESIDE,
        compiler_params=PARAMS,
    )(plain_v, plain_a, picked)

    for level in levels[:-1]:
        keep = terms.shape[0] // 2
        terms = terms[:keep] + lax.ppermute(terms[keep:], "src", xor_pairs(peers, bits[level]))
    came = lax.ppermute(terms[1], "src", xor_pairs(peers, bits[-1]))
    gradient = pl.pallas_call(
        gradient_kernel,
        out_shape=shaped(*log_conductivity.shape),
        in_specs=[VMEM] * 4,
        out_specs=VMEM,
        compiler_params=PARAMS,
    )(scale, prior, terms[0], came)
    return (field, adjoint, misfit, gradient)


def solution(mesh):
    in_specs = (
        P("src", None, "tile"),
        P("src", None, "tile"),
        P(),
        P(),
        P("src", None),
        P(),
        P("src", None),
        P("src", None, None, "tile"),
        P("src", None, None, "tile"),
    )
    out_specs = (
        P("src", None, None, "tile"),
        P("src", None, None, "tile"),
        P("src", None),
        P("src", None, "tile"),
    )
    return jax.shard_map(
        on_device, mesh=mesh, in_specs=in_specs, out_specs=out_specs, check_vma=False
    )
```

```python
import functools

import jax
import jax.numpy as jnp
from jax import lax
from jax.experimental import pallas as pl
from jax.experimental.pallas import tpu as pltpu
from jax.sharding import PartitionSpec as P

SWEEPS = 8
CLUSTERS = 4

LEAKAGE = 0.05
WEIGHT_X = 1.0
WEIGHT_Y = 0.5
WEIGHT_Z = 0.5
SMALLNESS = 1.0

GROUPS = 4
EDGE = SWEEPS + 1
SLOT = 32
HALF = SLOT // 2
PACK_AT = 1
TOGETHER = 8
DEPTH = 8

F32 = jnp.float32
BF16 = jnp.bfloat16
VMEM = pl.BlockSpec(memory_space=pltpu.VMEM)
SMEM = pl.BlockSpec(memory_space=pltpu.SMEM)
HBM = pl.BlockSpec(memory_space=pl.ANY)
BESIDE = pl.CostEstimate(flops=0, bytes_accessed=4_000_000, transcendentals=0)
PARAMS = pltpu.CompilerParams(vmem_limit_bytes=24 * 1024 * 1024)


def facing():
    return 1 - (lax.axis_index("tile") + lax.axis_index("src")) % 2


def xor_pairs(count, bit):
    return [(i, i ^ bit) for i in range(count)]


def lane_of(shape):
    return lax.broadcasted_iota(jnp.int32, shape, len(shape) - 1)


def depth_of(shape):
    return lax.broadcasted_iota(jnp.int32, shape, 0)


def turn(values, shift):
    return pltpu.roll(values, shift % 128, 1)


def up_depth(values):
    return pltpu.roll(values, values.shape[0] - 1, 0)


def down_depth(values):
    return pltpu.roll(values, 1, 0)


def full(value, shape):
    return jnp.full(shape, value, jnp.int32)


def each(count, body, unroll):
    def step(k, carry):
        body(k)
        return carry

    lax.fori_loop(0, count, step, 0, unroll=unroll)


def window(side, offset, shape):
    slot = ((lane_of(shape) - offset) & 127) % SLOT
    low = full(HALF - EDGE + EDGE * side, shape)
    return (slot >= low) & (slot < low + EDGE)


def joined(side, first, second, third):
    shape = first.shape
    out = jnp.where(window(side, 0, shape), first, turn(second, EDGE))
    return jnp.where(window(side, -EDGE, shape), turn(third, -EDGE), out)


def merge(pieces):
    group = lane_of(pieces[0].shape) // SLOT
    out = pieces[0]
    for g in range(1, GROUPS):
        out = jnp.where(group == g, pieces[g], out)
    return out


def rim_columns(shape, width):
    slot = lane_of(shape) % SLOT
    return HALF - 1 - slot + jnp.where(slot < HALF, width, 0)


def edges(row_of, k, per, shape):
    index = (HALF - 1 - lane_of(shape) % SLOT) & 127
    return merge([jnp.take_along_axis(row_of(k + per * g), index, axis=1) for g in range(GROUPS)])


def message_rows(per):
    return per + per // 2 + -(-(per // 2) // 3)


def model_place(k, per):
    if k < per // 2:
        return per + k, -EDGE
    k -= per // 2
    return per + per // 2 + k // 3, (0, EDGE, -EDGE)[k % 3]


def pack_fields_kernel(own_v, own_a, other_v, other_a, passed, payload, passed_on):
    del passed, passed_on
    per = own_v.shape[0] // GROUPS
    shape = own_v.shape[1:]
    side = facing()

    def part(ref, k):
        return edges(lambda y: ref[y], k, per, shape)

    def body(h):
        for k in (2 * h, 2 * h + 1):
            payload[k] = joined(side, part(own_v, k), part(other_v, k), part(own_a, k))
        first, second = part(other_a, 2 * h), part(other_a, 2 * h + 1)
        payload[per + h] = jnp.where(window(side, 0, shape), first, turn(second, EDGE))

    each(per // 2, body, 2)


def pack_model_kernel(order, gathered, part, payload, model):
    peers, rows_own = gathered.shape[:2]
    per = model.shape[0] // GROUPS
    shape = gathered.shape[2:]
    side = facing()
    for i in range(peers):
        j = sum(((i >> n) & 1) << bit for n, bit in enumerate(order))
        model[pl.ds((lax.axis_index("src") ^ j) * rows_own, rows_own)] = gathered[i]
    packed = [edges(lambda y: model[y], k, per, shape) for k in range(per)]
    half = per // 2
    for h in range(half):
        payload[per + h] = jnp.where(window(side, -EDGE, shape), turn(packed[h], -EDGE), part[per + h])
    for n, k in enumerate(range(half, per, 3)):
        payload[per + half + n] = joined(side, *[packed[min(k + m, per - 1)] for m in range(3)])


def own_field_kernel(
    total_x, cells, means, variances, labels, own_model, model, warm, observed,
    scale, prior, main, main_2, b_m, b_r, measured, nothing,
):
    rows, depth, width = warm.shape
    shape = (depth, width)
    per = rows // GROUPS
    first_col = lax.axis_index("tile") * width
    nothing[...] = jnp.zeros(nothing.shape, F32)
    measured[...] = jnp.where(full(first_col, observed.shape) == 0, observed[...], 0.0)
    m = own_model[...]
    label = labels[...]
    mean_cell = jnp.zeros(m.shape, F32)
    var_cell = jnp.zeros(m.shape, F32)
    for cluster in range(CLUSTERS):
        mean_cell = jnp.where(label == cluster, means[cluster], mean_cell)
        var_cell = jnp.where(label == cluster, variances[cluster], var_cell)
    scale[...] = -jnp.exp(m)
    prior[...] = SMALLNESS * (m - mean_cell) / var_cell

    def body(k):
        for g in range(GROUPS):
            y = k + per * g
            r = k + (per + 2) * g
            shift = SLOT * g + HALF
            put_row(main, r, turn(warm[y], shift))
            put_row(main_2, r, turn(jnp.exp(model[y]), shift))
            b_m[y] = jnp.zeros(shape, F32)
        b_r[k] = jnp.zeros(shape, F32)

    each(per, body, 2)
    clear_ends(main, per)
    clear_ends(main_2, per)
    lane, depth_at = lane_of(shape), depth_of(shape)
    for n, sign in ((0, 1.0), (1, -1.0)):
        cell = cells[0, n]
        line = cell // total_x
        x = cell - line * total_x
        y = line // depth
        g = y // per
        k = y - g * per
        at_depth = depth_at == line - y * depth
        col_m = first_col + ((lane - (SLOT * g + HALF)) & 127)
        b_m[y] = b_m[y] + jnp.where((col_m == x) & at_depth, sign, 0.0)
        at_slot = (first_col + columns(GROUPS, shape) == x) & (lane // SLOT == g)
        b_r[k] = b_r[k] + jnp.where(at_slot & at_depth, sign, 0.0)


def own_adjoint_kernel(mine, theirs, warm, spots, main, rim, hit_x):
    rows, depth, width = warm.shape
    per = rows // GROUPS
    mask = window(1 - facing(), 0, (depth, width))

    def body(h):
        for n in range(2):
            k = 2 * h + n
            for g in range(GROUPS):
                put_row(main, k + (per + 2) * g, turn(warm[k + per * g], SLOT * g + HALF))
            far = turn(theirs[per + h], -EDGE * n)
            put_row(rim, k, jnp.where(mask, turn(mine[k], EDGE), far))

    each(per // 2, body, 1)
    clear_ends(main, per)
    at = depth_of((2 * width, spots.shape[1]))
    slot = at % SLOT
    at = lax.axis_index("tile") * width + jnp.where(at < width, at, HALF - 1 - slot + jnp.where(slot < HALF, width, 0))
    hit_x[...] = jnp.where(at == spots[0:1, :], 1.0, 0.0).astype(BF16)


def save_kernel(field, adjoint, misfit, field_out, adjoint_out, misfit_out, sems):
    pairs = ((field, field_out.at[0]), (adjoint, adjoint_out.at[0]), (misfit, misfit_out))
    copies = [pltpu.make_async_copy(a, b, sems.at[n]) for n, (a, b) in enumerate(pairs)]
    for copy in copies:
        copy.start()
    for copy in copies:
        copy.wait()


def at_row(ref, y, shift=0):
    return ref[(y + 1) * DEPTH + shift : (y + 2) * DEPTH + shift, :]


def put_row(ref, y, values):
    start = (y + 1) * DEPTH
    if not isinstance(y, int):
        start = pl.multiple_of(start, DEPTH)
    ref[pl.ds(start, DEPTH), :] = values


def row_set(main, rim, k, per):
    return [at_row(main, g * (per + 2) + k) for g in range(GROUPS)] + [at_row(rim, k)]


def beside(own):
    packed = own[GROUPS]
    lane = lane_of(packed.shape)
    slot = lane % SLOT
    before, after = [], []
    for g in range(GROUPS):
        last = SLOT * g + HALF - 1
        after.append(jnp.where(lane == last, packed, turn(own[g], -1)))
        before.append(jnp.where(lane == last + 1, packed, turn(own[g], 1)))
    inner = merge(own[:GROUPS])
    before.append(jnp.where(slot == HALF - 1, inner, turn(packed, -1)))
    after.append(jnp.where(slot == HALF, inner, turn(packed, 1)))
    return before, after


def wrap(main, rim, per):
    put_row(rim, -1, turn(at_row(rim, per - 1), SLOT))
    put_row(rim, per, turn(at_row(rim, 0), -SLOT))
    for g in range(1, GROUPS):
        start = g * (per + 2)
        put_row(main, start - 1, turn(at_row(main, start - 3), SLOT))
        put_row(main, start - 2, turn(at_row(main, start), -SLOT))


def clear_ends(main, per):
    put_row(main, -1, jnp.zeros((DEPTH, main.shape[1]), F32))
    put_row(main, GROUPS * (per + 2) - 2, jnp.zeros((DEPTH, main.shape[1]), F32))


def sweep(old, new, face_m, face_r, b_m, b_r, first):
    per = b_r.shape[0]
    for step in range(per):
        k = (first + step) % per
        if step == 0 or k == 0:
            above, own = row_set(*old, k - 1, per), row_set(*old, k, per)
            face_above = [face_m[2, (per + 1) * g + k] for g in range(GROUPS)] + [face_r[2, k]]
        else:
            above, own = own, below
        below = row_set(*old, k + 1, per)
        before, after = beside(own)
        done = []
        for g in range(GROUPS + 1):
            n = g // GROUPS
            face, b = ((face_m, face_r)[n], (b_m, b_r)[n])
            y = k if n else k + per * g
            r = k if n else k + (per + 2) * g
            c = k if n else k + (per + 1) * g
            fy, fz = face[2, c + 1], face[3, c + 1]
            total = b[y] + face[0, c + 1] * after[g] + face[1, c + 1] * before[g]
            total = total + (fz * up_depth(own[g]) + down_depth(fz * own[g]))
            total = total + (fy * below[g] + face_above[g] * above[g])
            face_above[g] = fy
            done.append(total * face[4, c + 1])
            put_row(new[n], r, done[g])
        if k == 0:
            put_row(new[1], per, turn(done[GROUPS], -SLOT))
            for g in range(1, GROUPS):
                put_row(new[0], g * (per + 2) - 2, turn(done[g], -SLOT))
        if k == per - 1:
            put_row(new[1], -1, turn(done[GROUPS], SLOT))
            for g in range(1, GROUPS):
                put_row(new[0], g * (per + 2) - 1, turn(done[g - 1], SLOT))


def relax(first, second, face_m, face_r, b_m, b_r):
    per = b_r.shape[0]
    clear_ends(second[0], per)
    wrap(*first, per)

    def some(_, carry):
        for n in range(TOGETHER):
            old, new = (first, second) if n % 2 == 0 else (second, first)
            sweep(old, new, face_m, face_r, b_m, b_r, n)
        return carry

    lax.fori_loop(0, SWEEPS // TOGETHER, some, 0)


def three_parts(values):
    high = values.astype(BF16)
    rest = values - high.astype(F32)
    middle = rest.astype(BF16)
    low = (rest - middle.astype(F32)).astype(BF16)
    return high, middle, low


def columns(g, shape):
    if g == GROUPS:
        return rim_columns(shape, shape[1])
    return (lane_of(shape) - (SLOT * g + HALF)) & 127


def coefficients(total_x, first_col, main, rim, face_m, face_r):
    per = face_r.shape[1] - 1
    rows = per * GROUPS
    shape = face_r.shape[2:]
    group = lane_of(shape) // SLOT
    bottom = depth_of(shape) == shape[0] - 1
    for k in range(per):
        own = row_set(main, rim, k, per)
        before, after = beside(own)
        for g in range(GROUPS + 1):
            n = g // GROUPS
            field, face = ((main, rim)[n], (face_m, face_r)[n])
            y = k if n else k + per * g
            r = k if n else k + (per + 2) * g
            c = k if n else k + (per + 1) * g
            col = first_col + columns(g, shape)
            s = own[g]
            fx = jnp.where((col == total_x - 1) | (col == -1), 0.0, WEIGHT_X * 0.5 * (s + after[g]))
            bx = jnp.where((col == 0) | (col == total_x), 0.0, WEIGHT_X * 0.5 * (before[g] + s))
            fz = jnp.where(bottom, 0.0, WEIGHT_Z * 0.5 * (s + up_depth(s)))
            bz = down_depth(fz)
            fy = WEIGHT_Y * 0.5 * (s + at_row(field, r + 1))
            by = WEIGHT_Y * 0.5 * (at_row(field, r - 1) + s)
            if n and k == 0:
                by = jnp.where(group == 0, 0.0, by)
            if n and k == per - 1:
                fy = jnp.where(group == GROUPS - 1, 0.0, fy)
            if not n and y == 0:
                by = jnp.zeros(shape, F32)
            if not n and y == rows - 1:
                fy = jnp.zeros(shape, F32)
            diagonal = fx + bx + fy + by + fz + bz + LEAKAGE * s
            face[0, c + 1] = fx
            face[1, c + 1] = bx
            face[2, c + 1] = fy
            if not n and k == 0:
                face[2, c] = by
            face[3, c + 1] = fz
            face[4, c + 1] = 1.0 / diagonal
    face_r[2, 0] = turn(face_r[2, per], SLOT)


def field_kernel(
    total_x, mine, theirs, main_in, sigma_in, b_m, b_r, spots, measured,
    picked, plain, main, rim, face_m, face_r, main_2, rim_2,
):
    del main_in, sigma_in
    rows, depth, width = plain.shape
    shape = (depth, width)
    per = rows // GROUPS
    first_col = lax.axis_index("tile") * width
    mask = window(1 - facing(), 0, shape)
    filled = mask | window(facing(), 0, shape)
    for k in range(per):
        put_row(rim, k, jnp.where(mask, mine[k], turn(theirs[k], -EDGE)))
        row, offset = model_place(k, per)
        beyond = turn(jnp.where(window(1 - facing(), offset, shape), mine[row], theirs[row]), -offset)
        put_row(rim_2, k, jnp.exp(jnp.where(filled, beyond, 0.0)))
    wrap(main_2, rim_2, per)
    coefficients(total_x, first_col, main_2, rim_2, face_m, face_r)
    relax((main, rim), (main_2, rim_2), face_m, face_r, b_m, b_r)
    for y in range(rows):
        plain[y] = turn(at_row(main, y + 2 * (y // per)), -(SLOT * (y // per) + HALF))
    count = spots.shape[1]
    x_row = spots[0:1, :] - first_col
    line_row = spots[1:2, :]
    hit_x = jnp.where(depth_of((width, count)) == x_row, 1.0, 0.0).astype(BF16)
    flat = plain[...].reshape(rows * depth, width)
    lines = sum(jnp.dot(part, hit_x, preferred_element_type=F32) for part in three_parts(flat))
    hit_line = depth_of((rows * depth, count)) == line_row
    got = jnp.sum(jnp.where(hit_line, lines, 0.0), axis=0, keepdims=True)
    picked[...] = got[:, : count // 2] - got[:, count // 2 :] - measured[...]


def adjoint_kernel(
    total_x, places, picked, spots, main_in, rim_in, hit_x, main_v, rim_v, face_m, face_r,
    terms, plain, main, rim, main_2, rim_2, b_m, b_r,
):
    del main_in, rim_in
    rows, depth, width = plain.shape
    shape = (depth, width)
    per = rows // GROUPS
    me = lax.axis_index("src")
    first_col = lax.axis_index("tile") * width
    count = spots.shape[1]
    misfit = picked[...]
    weights = jnp.concatenate([misfit, -misfit], axis=1)
    hit_line = depth_of((rows * depth, count)) == spots[1:2, :]
    flat = jnp.zeros((rows * depth, 2 * width), F32)
    for part in three_parts(weights):
        left = jnp.where(hit_line, part.astype(F32), 0.0).astype(BF16)
        flat = flat + lax.dot_general(left, hit_x[...], (((1,), (1,)), ((), ())), preferred_element_type=F32)
    flat = flat.reshape(rows, depth, 2 * width)
    for y in range(rows):
        b_m[y] = turn(flat[y, :, :width], SLOT * (y // per) + HALF)
    for k in range(per):
        b_r[k] = merge([flat[k + per * g, :, width:] for g in range(GROUPS)])
    relax((main, rim), (main_2, rim_2), face_m, face_r, b_m, b_r)
    for y in range(rows):
        plain[y] = turn(at_row(main, y + 2 * (y // per)), -(SLOT * (y // per) + HALF))
    rows_own = terms.shape[1]
    bottom = depth_of(shape) == depth - 1
    for k in range(per):
        f_own, a_own = row_set(main_v, rim_v, k, per), row_set(main, rim, k, per)
        f_before, f_after = beside(f_own)
        a_before, a_after = beside(a_own)
        for g in range(GROUPS):
            y, r = k + per * g, k + (per + 2) * g
            col = first_col + columns(g, shape)
            f, a = f_own[g], a_own[g]
            px_next = jnp.where(col == total_x - 1, 0.0, (f_after[g] - f) * (a_after[g] - a))
            px_prev = jnp.where(col == 0, 0.0, (f - f_before[g]) * (a - a_before[g]))
            py = jnp.zeros(shape, F32)
            if y + 1 < rows:
                py = py + (at_row(main_v, r + 1) - f) * (at_row(main, r + 1) - a)
            if y > 0:
                py = py + (f - at_row(main_v, r - 1)) * (a - at_row(main, r - 1))
            pz = jnp.where(bottom, 0.0, (at_row(main_v, r, 1) - f) * (at_row(main, r, 1) - a))
            pz = pz + down_depth(pz)
            paired = WEIGHT_X * (px_prev + px_next) + WEIGHT_Y * py + WEIGHT_Z * pz
            j = me ^ (y // rows_own)
            place = sum(((j >> bit) & 1) << n for n, bit in enumerate(reversed(places)))
            term = 0.5 * paired + LEAKAGE * f * a
            terms[place, y % rows_own] = turn(term, -(SLOT * g + HALF))


def gradient_kernel(scale, prior, kept, came, gradient):
    gradient[...] = scale[...] * (kept[...] + came[...]) + prior[...]


def on_device(
    log_conductivity,
    cluster_labels,
    cluster_means,
    cluster_vars,
    source_cells,
    receiver_cells,
    observed,
    warm_potential,
    warm_adjoint,
):
    tile, src = lax.axis_index("tile"), lax.axis_index("src")
    tiles, peers = lax.axis_size("tile"), lax.axis_size("src")
    rows_own, depth, width = log_conductivity.shape
    rows = rows_own * peers
    per = rows // GROUPS
    total_x = width * tiles
    receivers = receiver_cells.shape[0]
    bits = [1 << n for n in range(peers.bit_length() - 1)]
    levels = list(range(len(bits)))
    spots = receiver_cells.T.reshape(1, 2 * receivers)
    spots = jnp.concatenate([spots % total_x, spots // total_x], axis=0)
    spots = jnp.pad(spots, ((0, 6), (0, 0)), constant_values=-1)
    start_v, start_a = warm_potential[0], warm_adjoint[0]

    def shaped(*sizes):
        return jax.ShapeDtypeStruct(sizes, F32)

    other_v = lax.ppermute(start_v, "src", xor_pairs(peers, 1))
    other_a = lax.ppermute(start_a, "src", xor_pairs(peers, 1))
    order = levels[:0:-1] + [0]
    own = log_conductivity[None]
    gathered = lax.optimization_barrier(jnp.pad(own, ((0, peers - 1), (0, 0), (0, 0), (0, 0))))
    for n, level in enumerate(order):
        sent = own if n == 0 else gathered[: 1 << n]
        came = lax.ppermute(sent, "src", xor_pairs(peers, bits[level]))
        if n == PACK_AT:
            payload, gathered = pl.pallas_call(
                pack_fields_kernel,
                out_shape=(shaped(message_rows(per), depth, width), shaped(*gathered.shape)),
                in_specs=[VMEM] * 5,
                out_specs=(VMEM, VMEM),
                input_output_aliases={4: 1},
                cost_estimate=BESIDE,
                compiler_params=PARAMS,
            )(start_v, start_a, other_v, other_a, gathered)
        gathered = lax.dynamic_update_slice(gathered, came, (1 << n, 0, 0, 0))
    payload, model = pl.pallas_call(
        functools.partial(pack_model_kernel, order),
        out_shape=(shaped(*payload.shape), shaped(rows, depth, width)),
        in_specs=[VMEM, VMEM],
        out_specs=(VMEM, VMEM),
        input_output_aliases={1: 0},
        compiler_params=PARAMS,
    )(gathered, payload)
    pairs = []
    for t in range(tiles):
        for s in range(peers):
            t_to = (t + 1) % tiles if (t + s) % 2 == 0 else (t - 1) % tiles
            pairs.append((t * peers + s, t_to * peers + s))
    mine = lax.ppermute(payload, ("tile", "src"), pairs)
    main_shape, rim_shape = ((rows + 2 * GROUPS) * depth, width), ((per + 2) * depth, width)
    scale, prior, main_v, sigma, b_m, b_r, measured, nothing = pl.pallas_call(
        functools.partial(own_field_kernel, total_x),
        out_shape=(shaped(*log_conductivity.shape),) * 2
        + (shaped(*main_shape),) * 2
        + (
            shaped(rows, depth, width),
            shaped(per, depth, width),
            shaped(*observed.shape),
            shaped(1, depth, width),
        ),
        in_specs=[SMEM] * 3 + [VMEM] * 5,
        out_specs=(VMEM,) * 8,
        cost_estimate=BESIDE,
        compiler_params=PARAMS,
    )(
        source_cells, cluster_means, cluster_vars, cluster_labels, log_conductivity,
        model, start_v, observed,
    )
    theirs = lax.ppermute(mine + nothing, "src", xor_pairs(peers, 1))
    picked, plain_v, main_v, rim_v, face_m, face_r, _ = pl.pallas_call(
        functools.partial(field_kernel, total_x),
        out_shape=(
            shaped(1, receivers),
            shaped(rows, depth, width),
            shaped(*main_shape),
            shaped(*rim_shape),
            shaped(5, rows + GROUPS, depth, width),
            shaped(5, per + 1, depth, width),
            shaped(*main_shape),
        ),
        in_specs=[VMEM] * 8,
        out_specs=(VMEM,) * 7,
        input_output_aliases={2: 2, 3: 6},
        scratch_shapes=[pltpu.VMEM(rim_shape, F32)],
        compiler_params=PARAMS,
    )(mine, theirs, main_v, sigma, b_m, b_r, spots, measured)
    main_a, rim_a, hit_x = pl.pallas_call(
        own_adjoint_kernel,
        out_shape=(
            shaped(*main_shape),
            shaped(*rim_shape),
            jax.ShapeDtypeStruct((2 * width, 2 * receivers), BF16),
        ),
        in_specs=[VMEM] * 4,
        out_specs=(VMEM,) * 3,
        cost_estimate=BESIDE,
        compiler_params=PARAMS,
    )(mine, theirs, start_a, spots)

    step = 1
    while step < tiles:
        picked = picked + lax.ppermute(picked, "tile", xor_pairs(tiles, step))
        step *= 2

    terms, plain_a, _, _ = pl.pallas_call(
        functools.partial(adjoint_kernel, total_x, levels),
        out_shape=(
            shaped(peers, rows_own, depth, width),
            shaped(rows, depth, width),
            shaped(*main_shape),
            shaped(*rim_shape),
        ),
        in_specs=[VMEM] * 9,
        out_specs=(VMEM,) * 4,
        input_output_aliases={2: 2, 3: 3},
        scratch_shapes=[
            pltpu.VMEM(main_shape, F32),
            pltpu.VMEM(rim_shape, F32),
            pltpu.VMEM((rows, depth, width), F32),
            pltpu.VMEM((per, depth, width), F32),
        ],
        compiler_params=PARAMS,
    )(picked, spots, main_a, rim_a, hit_x, main_v, rim_v, face_m, face_r)
    field, adjoint, misfit = pl.pallas_call(
        save_kernel,
        out_shape=(shaped(*warm_potential.shape), shaped(*warm_adjoint.shape), shaped(*observed.shape)),
        in_specs=[VMEM] * 3,
        out_specs=(HBM,) * 3,
        scratch_shapes=[pltpu.SemaphoreType.DMA((3,))],
        cost_estimate=BESIDE,
        compiler_params=PARAMS,
    )(plain_v, plain_a, picked)

    for level in levels[:-1]:
        keep = terms.shape[0] // 2
        terms = terms[:keep] + lax.ppermute(terms[keep:], "src", xor_pairs(peers, bits[level]))
    came = lax.ppermute(terms[1], "src", xor_pairs(peers, bits[-1]))
    gradient = pl.pallas_call(
        gradient_kernel,
        out_shape=shaped(*log_conductivity.shape),
        in_specs=[VMEM] * 4,
        out_specs=VMEM,
        compiler_params=PARAMS,
    )(scale, prior, terms[0], came)
    return (field, adjoint, misfit, gradient)


def solution(mesh):
    in_specs = (
        P("src", None, "tile"),
        P("src", None, "tile"),
        P(),
        P(),
        P("src", None),
        P(),
        P("src", None),
        P("src", None, None, "tile"),
        P("src", None, None, "tile"),
    )
    out_specs = (
        P("src", None, None, "tile"),
        P("src", None, None, "tile"),
        P("src", None),
        P("src", None, "tile"),
    )
    return jax.shard_map(
        on_device, mesh=mesh, in_specs=in_specs, out_specs=out_specs, check_vma=False
    )
```

```python
import functools

import jax
import jax.numpy as jnp
from jax import lax
from jax.experimental import pallas as pl
from jax.experimental.pallas import tpu as pltpu
from jax.sharding import PartitionSpec as P

SWEEPS = 8
CLUSTERS = 4

LEAKAGE = 0.05
WEIGHT_X = 1.0
WEIGHT_Y = 0.5
WEIGHT_Z = 0.5
SMALLNESS = 1.0

GROUPS = 4
EDGE = SWEEPS + 1
SLOT = 32
HALF = SLOT // 2
PACK_AT = 1
TOGETHER = 8
DEPTH = 8

F32 = jnp.float32
BF16 = jnp.bfloat16
VMEM = pl.BlockSpec(memory_space=pltpu.VMEM)
SMEM = pl.BlockSpec(memory_space=pltpu.SMEM)
HBM = pl.BlockSpec(memory_space=pl.ANY)
BESIDE = pl.CostEstimate(flops=0, bytes_accessed=4_000_000, transcendentals=0)
PARAMS = pltpu.CompilerParams(vmem_limit_bytes=24 * 1024 * 1024)


def facing():
    return 1 - (lax.axis_index("tile") + lax.axis_index("src")) % 2


def xor_pairs(count, bit):
    return [(i, i ^ bit) for i in range(count)]


def lane_of(shape):
    return lax.broadcasted_iota(jnp.int32, shape, len(shape) - 1)


def depth_of(shape):
    return lax.broadcasted_iota(jnp.int32, shape, 0)


def turn(values, shift):
    return pltpu.roll(values, shift % 128, 1)


def up_depth(values):
    return pltpu.roll(values, values.shape[0] - 1, 0)


def down_depth(values):
    return pltpu.roll(values, 1, 0)


def full(value, shape):
    return jnp.full(shape, value, jnp.int32)


def each(count, body, unroll):
    def step(k, carry):
        body(k)
        return carry

    lax.fori_loop(0, count, step, 0, unroll=unroll)


def window(side, offset, shape):
    slot = ((lane_of(shape) - offset) & 127) % SLOT
    low = full(HALF - EDGE + EDGE * side, shape)
    return (slot >= low) & (slot < low + EDGE)


def joined(side, first, second, third):
    shape = first.shape
    out = jnp.where(window(side, 0, shape), first, turn(second, EDGE))
    return jnp.where(window(side, -EDGE, shape), turn(third, -EDGE), out)


def merge(pieces):
    group = lane_of(pieces[0].shape) // SLOT
    out = pieces[0]
    for g in range(1, GROUPS):
        out = jnp.where(group == g, pieces[g], out)
    return out


def rim_columns(shape, width):
    slot = lane_of(shape) % SLOT
    return HALF - 1 - slot + jnp.where(slot < HALF, width, 0)


def edges(row_of, k, per, shape):
    index = (HALF - 1 - lane_of(shape) % SLOT) & 127
    return merge([jnp.take_along_axis(row_of(k + per * g), index, axis=1) for g in range(GROUPS)])


def message_rows(per):
    return per + per // 2 + -(-(per // 2) // 3)


def model_place(k, per):
    if k < per // 2:
        return per + k, -EDGE
    k -= per // 2
    return per + per // 2 + k // 3, (0, EDGE, -EDGE)[k % 3]


def pack_fields_kernel(own_v, own_a, other_v, other_a, passed, payload, passed_on):
    del passed, passed_on
    per = own_v.shape[0] // GROUPS
    shape = own_v.shape[1:]
    side = facing()

    def part(ref, k):
        return edges(lambda y: ref[y], k, per, shape)

    def body(h):
        for k in (2 * h, 2 * h + 1):
            payload[k] = joined(side, part(own_v, k), part(other_v, k), part(own_a, k))
        first, second = part(other_a, 2 * h), part(other_a, 2 * h + 1)
        payload[per + h] = jnp.where(window(side, 0, shape), first, turn(second, EDGE))

    each(per // 2, body, 2)


def pack_model_kernel(order, gathered, part, payload, model):
    peers, rows_own = gathered.shape[:2]
    per = model.shape[0] // GROUPS
    shape = gathered.shape[2:]
    side = facing()
    for i in range(peers):
        j = sum(((i >> n) & 1) << bit for n, bit in enumerate(order))
        model[pl.ds((lax.axis_index("src") ^ j) * rows_own, rows_own)] = gathered[i]
    packed = [edges(lambda y: model[y], k, per, shape) for k in range(per)]
    half = per // 2
    for h in range(half):
        payload[per + h] = jnp.where(window(side, -EDGE, shape), turn(packed[h], -EDGE), part[per + h])
    for n, k in enumerate(range(half, per, 3)):
        payload[per + half + n] = joined(side, *[packed[min(k + m, per - 1)] for m in range(3)])


def own_field_kernel(
    total_x, cells, means, variances, labels, own_model, model, warm, observed,
    scale, prior, main, main_2, b_m, b_r, measured, nothing,
):
    rows, depth, width = warm.shape
    shape = (depth, width)
    per = rows // GROUPS
    first_col = lax.axis_index("tile") * width
    nothing[...] = jnp.zeros(nothing.shape, F32)
    measured[...] = jnp.where(full(first_col, observed.shape) == 0, observed[...], 0.0)
    m = own_model[...]
    label = labels[...]
    mean_cell = jnp.zeros(m.shape, F32)
    var_cell = jnp.zeros(m.shape, F32)
    for cluster in range(CLUSTERS):
        mean_cell = jnp.where(label == cluster, means[cluster], mean_cell)
        var_cell = jnp.where(label == cluster, variances[cluster], var_cell)
    scale[...] = -jnp.exp(m)
    prior[...] = SMALLNESS * (m - mean_cell) / var_cell

    def body(k):
        for g in range(GROUPS):
            y = k + per * g
            r = k + (per + 2) * g
            shift = SLOT * g + HALF
            put_row(main, r, turn(warm[y], shift))
            put_row(main_2, r, turn(jnp.exp(model[y]), shift))
            b_m[y] = jnp.zeros(shape, F32)
        b_r[k] = jnp.zeros(shape, F32)

    each(per, body, 2)
    clear_ends(main, per)
    clear_ends(main_2, per)
    lane, depth_at = lane_of(shape), depth_of(shape)
    for n, sign in ((0, 1.0), (1, -1.0)):
        cell = cells[0, n]
        line = cell // total_x
        x = cell - line * total_x
        y = line // depth
        g = y // per
        k = y - g * per
        at_depth = depth_at == line - y * depth
        col_m = first_col + ((lane - (SLOT * g + HALF)) & 127)
        b_m[y] = b_m[y] + jnp.where((col_m == x) & at_depth, sign, 0.0)
        at_slot = (first_col + columns(GROUPS, shape) == x) & (lane // SLOT == g)
        b_r[k] = b_r[k] + jnp.where(at_slot & at_depth, sign, 0.0)


def turned_place(spots, first_col, width):
    x = spots[0:1, :] - first_col
    return jnp.where((x >= 0) & (x < width), (x + SLOT * spots[2:3, :] + HALF) & 127, -1)


def own_adjoint_kernel(mine, theirs, warm, spots, main, rim, hit_x):
    rows, depth, width = warm.shape
    per = rows // GROUPS
    mask = window(1 - facing(), 0, (depth, width))

    def body(h):
        for n in range(2):
            k = 2 * h + n
            for g in range(GROUPS):
                put_row(main, k + (per + 2) * g, turn(warm[k + per * g], SLOT * g + HALF))
            far = turn(theirs[per + h], -EDGE * n)
            put_row(rim, k, jnp.where(mask, turn(mine[k], EDGE), far))

    each(per // 2, body, 1)
    clear_ends(main, per)
    first_col = lax.axis_index("tile") * width
    at = depth_of((width, spots.shape[1]))
    slot = at % SLOT
    rim_at = first_col + HALF - 1 - slot + jnp.where(slot < HALF, width, 0)
    hit_x[:width, :] = jnp.where(at == turned_place(spots, first_col, width), 1.0, 0.0).astype(BF16)
    hit_x[width:, :] = jnp.where(rim_at == spots[0:1, :], 1.0, 0.0).astype(BF16)


def save_kernel(field, adjoint, misfit, field_out, adjoint_out, misfit_out, plain_v, plain_a, sems):
    copies = [pltpu.make_async_copy(misfit, misfit_out, sems.at[2])]
    copies[0].start()
    rows = plain_v.shape[0]
    per = rows // GROUPS
    for n, (main, plain, out) in enumerate(((field, plain_v, field_out), (adjoint, plain_a, adjoint_out))):
        for y in range(rows):
            g = y // per
            plain[y] = turn(at_row(main, y + 2 * g), -(SLOT * g + HALF))
        copies.append(pltpu.make_async_copy(plain, out.at[0], sems.at[n]))
        copies[-1].start()
    for copy in copies:
        copy.wait()


def at_row(ref, y, shift=0):
    return ref[(y + 1) * DEPTH + shift : (y + 2) * DEPTH + shift, :]


def put_row(ref, y, values):
    start = (y + 1) * DEPTH
    if not isinstance(y, int):
        start = pl.multiple_of(start, DEPTH)
    ref[pl.ds(start, DEPTH), :] = values


def row_set(main, rim, k, per):
    return [at_row(main, g * (per + 2) + k) for g in range(GROUPS)] + [at_row(rim, k)]


def beside(own):
    packed = own[GROUPS]
    lane = lane_of(packed.shape)
    slot = lane % SLOT
    before, after = [], []
    for g in range(GROUPS):
        last = SLOT * g + HALF - 1
        after.append(jnp.where(lane == last, packed, turn(own[g], -1)))
        before.append(jnp.where(lane == last + 1, packed, turn(own[g], 1)))
    inner = merge(own[:GROUPS])
    before.append(jnp.where(slot == HALF - 1, inner, turn(packed, -1)))
    after.append(jnp.where(slot == HALF, inner, turn(packed, 1)))
    return before, after


def wrap(main, rim, per):
    put_row(rim, -1, turn(at_row(rim, per - 1), SLOT))
    put_row(rim, per, turn(at_row(rim, 0), -SLOT))
    for g in range(1, GROUPS):
        start = g * (per + 2)
        put_row(main, start - 1, turn(at_row(main, start - 3), SLOT))
        put_row(main, start - 2, turn(at_row(main, start), -SLOT))


def clear_ends(main, per):
    put_row(main, -1, jnp.zeros((DEPTH, main.shape[1]), F32))
    put_row(main, GROUPS * (per + 2) - 2, jnp.zeros((DEPTH, main.shape[1]), F32))


def sweep(old, new, face_m, face_r, b_m, b_r, first):
    per = b_r.shape[0]
    for step in range(per):
        k = (first + step) % per
        if step == 0 or k == 0:
            above, own = row_set(*old, k - 1, per), row_set(*old, k, per)
            face_above = [face_m[2, (per + 1) * g + k] for g in range(GROUPS)] + [face_r[2, k]]
        else:
            above, own = own, below
        below = row_set(*old, k + 1, per)
        before, after = beside(own)
        done = []
        for g in range(GROUPS + 1):
            n = g // GROUPS
            face, b = ((face_m, face_r)[n], (b_m, b_r)[n])
            y = k if n else k + per * g
            r = k if n else k + (per + 2) * g
            c = k if n else k + (per + 1) * g
            fy, fz = face[2, c + 1], face[3, c + 1]
            total = b[y] + face[0, c + 1] * after[g] + face[1, c + 1] * before[g]
            total = total + (fz * up_depth(own[g]) + down_depth(fz * own[g]))
            total = total + (fy * below[g] + face_above[g] * above[g])
            face_above[g] = fy
            done.append(total * face[4, c + 1])
            put_row(new[n], r, done[g])
        if k == 0:
            put_row(new[1], per, turn(done[GROUPS], -SLOT))
            for g in range(1, GROUPS):
                put_row(new[0], g * (per + 2) - 2, turn(done[g], -SLOT))
        if k == per - 1:
            put_row(new[1], -1, turn(done[GROUPS], SLOT))
            for g in range(1, GROUPS):
                put_row(new[0], g * (per + 2) - 1, turn(done[g - 1], SLOT))


def relax(first, second, face_m, face_r, b_m, b_r):
    per = b_r.shape[0]
    clear_ends(second[0], per)
    wrap(*first, per)

    def some(_, carry):
        for n in range(TOGETHER):
            old, new = (first, second) if n % 2 == 0 else (second, first)
            sweep(old, new, face_m, face_r, b_m, b_r, n)
        return carry

    lax.fori_loop(0, SWEEPS // TOGETHER, some, 0)


def three_parts(values):
    high = values.astype(BF16)
    rest = values - high.astype(F32)
    middle = rest.astype(BF16)
    low = (rest - middle.astype(F32)).astype(BF16)
    return high, middle, low


def columns(g, shape):
    if g == GROUPS:
        return rim_columns(shape, shape[1])
    return (lane_of(shape) - (SLOT * g + HALF)) & 127


def coefficients(total_x, first_col, main, rim, face_m, face_r):
    per = face_r.shape[1] - 1
    rows = per * GROUPS
    shape = face_r.shape[2:]
    group = lane_of(shape) // SLOT
    bottom = depth_of(shape) == shape[0] - 1
    for k in range(per):
        own = row_set(main, rim, k, per)
        before, after = beside(own)
        for g in range(GROUPS + 1):
            n = g // GROUPS
            field, face = ((main, rim)[n], (face_m, face_r)[n])
            y = k if n else k + per * g
            r = k if n else k + (per + 2) * g
            c = k if n else k + (per + 1) * g
            col = first_col + columns(g, shape)
            s = own[g]
            fx = jnp.where((col == total_x - 1) | (col == -1), 0.0, WEIGHT_X * 0.5 * (s + after[g]))
            bx = jnp.where((col == 0) | (col == total_x), 0.0, WEIGHT_X * 0.5 * (before[g] + s))
            fz = jnp.where(bottom, 0.0, WEIGHT_Z * 0.5 * (s + up_depth(s)))
            bz = down_depth(fz)
            fy = WEIGHT_Y * 0.5 * (s + at_row(field, r + 1))
            by = WEIGHT_Y * 0.5 * (at_row(field, r - 1) + s)
            if n and k == 0:
                by = jnp.where(group == 0, 0.0, by)
            if n and k == per - 1:
                fy = jnp.where(group == GROUPS - 1, 0.0, fy)
            if not n and y == 0:
                by = jnp.zeros(shape, F32)
            if not n and y == rows - 1:
                fy = jnp.zeros(shape, F32)
            diagonal = fx + bx + fy + by + fz + bz + LEAKAGE * s
            face[0, c + 1] = fx
            face[1, c + 1] = bx
            face[2, c + 1] = fy
            if not n and k == 0:
                face[2, c] = by
            face[3, c + 1] = fz
            face[4, c + 1] = 1.0 / diagonal
    face_r[2, 0] = turn(face_r[2, per], SLOT)


def field_kernel(
    total_x, mine, theirs, main_in, sigma_in, b_m, b_r, spots, measured,
    picked, main, rim, face_m, face_r, main_2, rim_2,
):
    del main_in, sigma_in
    rows, depth, width = b_m.shape
    shape = (depth, width)
    per = rows // GROUPS
    first_col = lax.axis_index("tile") * width
    mask = window(1 - facing(), 0, shape)
    filled = mask | window(facing(), 0, shape)
    for k in range(per):
        put_row(rim, k, jnp.where(mask, mine[k], turn(theirs[k], -EDGE)))
        row, offset = model_place(k, per)
        beyond = turn(jnp.where(window(1 - facing(), offset, shape), mine[row], theirs[row]), -offset)
        put_row(rim_2, k, jnp.exp(jnp.where(filled, beyond, 0.0)))
    wrap(main_2, rim_2, per)
    coefficients(total_x, first_col, main_2, rim_2, face_m, face_r)
    relax((main, rim), (main_2, rim_2), face_m, face_r, b_m, b_r)
    count = spots.shape[1]
    line_row = spots[1:2, :]
    place = turned_place(spots, first_col, width)
    hit_x = jnp.where(depth_of((width, count)) == place, 1.0, 0.0).astype(BF16)
    starts = [(g * (per + 2) + 1) * depth for g in range(GROUPS)]
    flat = jnp.concatenate([main[start : start + per * depth, :] for start in starts], axis=0)
    lines = sum(jnp.dot(part, hit_x, preferred_element_type=F32) for part in three_parts(flat))
    hit_line = depth_of((rows * depth, count)) == line_row
    got = jnp.sum(jnp.where(hit_line, lines, 0.0), axis=0, keepdims=True)
    picked[...] = got[:, : count // 2] - got[:, count // 2 :] - measured[...]


def adjoint_kernel(
    total_x, places, picked, spots, main_in, rim_in, hit_x, main_v, rim_v, face_m, face_r,
    terms, main, rim, main_2, rim_2, b_m, b_r,
):
    del main_in, rim_in
    rows, depth, width = b_m.shape
    shape = (depth, width)
    per = rows // GROUPS
    me = lax.axis_index("src")
    first_col = lax.axis_index("tile") * width
    count = spots.shape[1]
    misfit = picked[...]
    weights = jnp.concatenate([misfit, -misfit], axis=1)
    hit_line = depth_of((rows * depth, count)) == spots[1:2, :]
    flat = jnp.zeros((rows * depth, 2 * width), F32)
    for part in three_parts(weights):
        left = jnp.where(hit_line, part.astype(F32), 0.0).astype(BF16)
        flat = flat + lax.dot_general(left, hit_x[...], (((1,), (1,)), ((), ())), preferred_element_type=F32)
    flat = flat.reshape(rows, depth, 2 * width)
    for y in range(rows):
        b_m[y] = flat[y, :, :width]
    for k in range(per):
        b_r[k] = merge([flat[k + per * g, :, width:] for g in range(GROUPS)])
    relax((main, rim), (main_2, rim_2), face_m, face_r, b_m, b_r)
    rows_own = terms.shape[1]
    bottom = depth_of(shape) == depth - 1
    for k in range(per):
        f_own, a_own = row_set(main_v, rim_v, k, per), row_set(main, rim, k, per)
        f_before, f_after = beside(f_own)
        a_before, a_after = beside(a_own)
        for g in range(GROUPS):
            y, r = k + per * g, k + (per + 2) * g
            col = first_col + columns(g, shape)
            f, a = f_own[g], a_own[g]
            px_next = jnp.where(col == total_x - 1, 0.0, (f_after[g] - f) * (a_after[g] - a))
            px_prev = jnp.where(col == 0, 0.0, (f - f_before[g]) * (a - a_before[g]))
            py = jnp.zeros(shape, F32)
            if y + 1 < rows:
                py = py + (at_row(main_v, r + 1) - f) * (at_row(main, r + 1) - a)
            if y > 0:
                py = py + (f - at_row(main_v, r - 1)) * (a - at_row(main, r - 1))
            pz = jnp.where(bottom, 0.0, (at_row(main_v, r, 1) - f) * (at_row(main, r, 1) - a))
            pz = pz + down_depth(pz)
            paired = WEIGHT_X * (px_prev + px_next) + WEIGHT_Y * py + WEIGHT_Z * pz
            j = me ^ (y // rows_own)
            place = sum(((j >> bit) & 1) << n for n, bit in enumerate(reversed(places)))
            term = 0.5 * paired + LEAKAGE * f * a
            terms[place, y % rows_own] = turn(term, -(SLOT * g + HALF))


def gradient_kernel(scale, prior, kept, came, gradient):
    gradient[...] = scale[...] * (kept[...] + came[...]) + prior[...]


def on_device(
    log_conductivity,
    cluster_labels,
    cluster_means,
    cluster_vars,
    source_cells,
    receiver_cells,
    observed,
    warm_potential,
    warm_adjoint,
):
    tile, src = lax.axis_index("tile"), lax.axis_index("src")
    tiles, peers = lax.axis_size("tile"), lax.axis_size("src")
    rows_own, depth, width = log_conductivity.shape
    rows = rows_own * peers
    per = rows // GROUPS
    total_x = width * tiles
    receivers = receiver_cells.shape[0]
    bits = [1 << n for n in range(peers.bit_length() - 1)]
    levels = list(range(len(bits)))
    spots = receiver_cells.T.reshape(1, 2 * receivers)
    line = spots // total_x
    spots = jnp.concatenate([spots % total_x, line, line // (depth * per)], axis=0)
    spots = jnp.pad(spots, ((0, 5), (0, 0)), constant_values=-1)
    start_v, start_a = warm_potential[0], warm_adjoint[0]

    def shaped(*sizes):
        return jax.ShapeDtypeStruct(sizes, F32)

    other_v = lax.ppermute(start_v, "src", xor_pairs(peers, 1))
    other_a = lax.ppermute(start_a, "src", xor_pairs(peers, 1))
    order = levels[:0:-1] + [0]
    own = log_conductivity[None]
    gathered = lax.optimization_barrier(jnp.pad(own, ((0, peers - 1), (0, 0), (0, 0), (0, 0))))
    for n, level in enumerate(order):
        sent = own if n == 0 else gathered[: 1 << n]
        came = lax.ppermute(sent, "src", xor_pairs(peers, bits[level]))
        if n == PACK_AT:
            payload, gathered = pl.pallas_call(
                pack_fields_kernel,
                out_shape=(shaped(message_rows(per), depth, width), shaped(*gathered.shape)),
                in_specs=[VMEM] * 5,
                out_specs=(VMEM, VMEM),
                input_output_aliases={4: 1},
                cost_estimate=BESIDE,
                compiler_params=PARAMS,
            )(start_v, start_a, other_v, other_a, gathered)
        gathered = lax.dynamic_update_slice(gathered, came, (1 << n, 0, 0, 0))
    payload, model = pl.pallas_call(
        functools.partial(pack_model_kernel, order),
        out_shape=(shaped(*payload.shape), shaped(rows, depth, width)),
        in_specs=[VMEM, VMEM],
        out_specs=(VMEM, VMEM),
        input_output_aliases={1: 0},
        compiler_params=PARAMS,
    )(gathered, payload)
    pairs = []
    for t in range(tiles):
        for s in range(peers):
            t_to = (t + 1) % tiles if (t + s) % 2 == 0 else (t - 1) % tiles
            pairs.append((t * peers + s, t_to * peers + s))
    mine = lax.ppermute(payload, ("tile", "src"), pairs)
    main_shape, rim_shape = ((rows + 2 * GROUPS) * depth, width), ((per + 2) * depth, width)
    scale, prior, main_v, sigma, b_m, b_r, measured, nothing = pl.pallas_call(
        functools.partial(own_field_kernel, total_x),
        out_shape=(shaped(*log_conductivity.shape),) * 2
        + (shaped(*main_shape),) * 2
        + (
            shaped(rows, depth, width),
            shaped(per, depth, width),
            shaped(*observed.shape),
            shaped(1, depth, width),
        ),
        in_specs=[SMEM] * 3 + [VMEM] * 5,
        out_specs=(VMEM,) * 8,
        cost_estimate=BESIDE,
        compiler_params=PARAMS,
    )(
        source_cells, cluster_means, cluster_vars, cluster_labels, log_conductivity,
        model, start_v, observed,
    )
    theirs = lax.ppermute(mine + nothing, "src", xor_pairs(peers, 1))
    picked, main_v, rim_v, face_m, face_r, _ = pl.pallas_call(
        functools.partial(field_kernel, total_x),
        out_shape=(
            shaped(1, receivers),
            shaped(*main_shape),
            shaped(*rim_shape),
            shaped(5, rows + GROUPS, depth, width),
            shaped(5, per + 1, depth, width),
            shaped(*main_shape),
        ),
        in_specs=[VMEM] * 8,
        out_specs=(VMEM,) * 6,
        input_output_aliases={2: 1, 3: 5},
        scratch_shapes=[pltpu.VMEM(rim_shape, F32)],
        compiler_params=PARAMS,
    )(mine, theirs, main_v, sigma, b_m, b_r, spots, measured)
    main_a, rim_a, hit_x = pl.pallas_call(
        own_adjoint_kernel,
        out_shape=(
            shaped(*main_shape),
            shaped(*rim_shape),
            jax.ShapeDtypeStruct((2 * width, 2 * receivers), BF16),
        ),
        in_specs=[VMEM] * 4,
        out_specs=(VMEM,) * 3,
        cost_estimate=BESIDE,
        compiler_params=PARAMS,
    )(mine, theirs, start_a, spots)

    step = 1
    while step < tiles:
        picked = picked + lax.ppermute(picked, "tile", xor_pairs(tiles, step))
        step *= 2

    terms, main_a, _ = pl.pallas_call(
        functools.partial(adjoint_kernel, total_x, levels),
        out_shape=(
            shaped(peers, rows_own, depth, width),
            shaped(*main_shape),
            shaped(*rim_shape),
        ),
        in_specs=[VMEM] * 9,
        out_specs=(VMEM,) * 3,
        input_output_aliases={2: 1, 3: 2},
        scratch_shapes=[
            pltpu.VMEM(main_shape, F32),
            pltpu.VMEM(rim_shape, F32),
            pltpu.VMEM((rows, depth, width), F32),
            pltpu.VMEM((per, depth, width), F32),
        ],
        compiler_params=PARAMS,
    )(picked, spots, main_a, rim_a, hit_x, main_v, rim_v, face_m, face_r)
    field, adjoint, misfit = pl.pallas_call(
        save_kernel,
        out_shape=(shaped(*warm_potential.shape), shaped(*warm_adjoint.shape), shaped(*observed.shape)),
        in_specs=[VMEM] * 3,
        out_specs=(HBM,) * 3,
        scratch_shapes=[pltpu.VMEM((rows, depth, width), F32)] * 2 + [pltpu.SemaphoreType.DMA((3,))],
        cost_estimate=BESIDE,
        compiler_params=PARAMS,
    )(main_v, main_a, picked)

    for level in levels[:-1]:
        keep = terms.shape[0] // 2
        terms = terms[:keep] + lax.ppermute(terms[keep:], "src", xor_pairs(peers, bits[level]))
    came = lax.ppermute(terms[1], "src", xor_pairs(peers, bits[-1]))
    gradient = pl.pallas_call(
        gradient_kernel,
        out_shape=shaped(*log_conductivity.shape),
        in_specs=[VMEM] * 4,
        out_specs=VMEM,
        compiler_params=PARAMS,
    )(scale, prior, terms[0], came)
    return (field, adjoint, misfit, gradient)


def solution(mesh):
    in_specs = (
        P("src", None, "tile"),
        P("src", None, "tile"),
        P(),
        P(),
        P("src", None),
        P(),
        P("src", None),
        P("src", None, None, "tile"),
        P("src", None, None, "tile"),
    )
    out_specs = (
        P("src", None, None, "tile"),
        P("src", None, None, "tile"),
        P("src", None),
        P("src", None, "tile"),
    )
    return jax.shard_map(
        on_device, mesh=mesh, in_specs=in_specs, out_specs=out_specs, check_vma=False
    )
```

```python
import functools

import jax
import jax.numpy as jnp
from jax import lax
from jax.experimental import pallas as pl
from jax.experimental.pallas import tpu as pltpu
from jax.sharding import PartitionSpec as P

SWEEPS = 8
CLUSTERS = 4

LEAKAGE = 0.05
WEIGHT_X = 1.0
WEIGHT_Y = 0.5
WEIGHT_Z = 0.5
SMALLNESS = 1.0

GROUPS = 4
EDGE = SWEEPS + 1
SLOT = 32
HALF = SLOT // 2
PACK_AT = 1
DEPTH = 8

F32 = jnp.float32
BF16 = jnp.bfloat16
VMEM = pl.BlockSpec(memory_space=pltpu.VMEM)
SMEM = pl.BlockSpec(memory_space=pltpu.SMEM)
HBM = pl.BlockSpec(memory_space=pl.ANY)
BESIDE = pl.CostEstimate(flops=0, bytes_accessed=4_000_000, transcendentals=0)
PARAMS = pltpu.CompilerParams(vmem_limit_bytes=24 * 1024 * 1024)


def facing():
    return 1 - (lax.axis_index("tile") + lax.axis_index("src")) % 2


def xor_pairs(count, bit):
    return [(i, i ^ bit) for i in range(count)]


def lane_of(shape):
    return lax.broadcasted_iota(jnp.int32, shape, len(shape) - 1)


def depth_of(shape):
    return lax.broadcasted_iota(jnp.int32, shape, 0)


def turn(values, shift):
    return pltpu.roll(values, shift % 128, 1)


def up_depth(values):
    return pltpu.roll(values, values.shape[0] - 1, 0)


def down_depth(values):
    return pltpu.roll(values, 1, 0)


def full(value, shape):
    return jnp.full(shape, value, jnp.int32)


def each(count, body, unroll):
    def step(k, carry):
        body(k)
        return carry

    lax.fori_loop(0, count, step, 0, unroll=unroll)


def window(side, offset, shape):
    slot = ((lane_of(shape) - offset) & 127) % SLOT
    low = full(HALF - EDGE + EDGE * side, shape)
    return (slot >= low) & (slot < low + EDGE)


def joined(side, first, second, third):
    shape = first.shape
    out = jnp.where(window(side, 0, shape), first, turn(second, EDGE))
    return jnp.where(window(side, -EDGE, shape), turn(third, -EDGE), out)


def merge(pieces):
    group = lane_of(pieces[0].shape) // SLOT
    out = pieces[0]
    for g in range(1, GROUPS):
        out = jnp.where(group == g, pieces[g], out)
    return out


def rim_columns(shape, width):
    slot = lane_of(shape) % SLOT
    return HALF - 1 - slot + jnp.where(slot < HALF, width, 0)


def edges(row_of, k, per, shape):
    index = (HALF - 1 - lane_of(shape) % SLOT) & 127
    return merge([jnp.take_along_axis(row_of(k + per * g), index, axis=1) for g in range(GROUPS)])


def message_rows(per):
    return per + per // 2 + -(-(per // 2) // 3)


def model_place(k, per):
    if k < per // 2:
        return per + k, -EDGE
    k -= per // 2
    return per + per // 2 + k // 3, (0, EDGE, -EDGE)[k % 3]


def pack_fields_kernel(own_v, own_a, other_v, other_a, passed, payload, passed_on):
    del passed, passed_on
    per = own_v.shape[0] // GROUPS
    shape = own_v.shape[1:]
    side = facing()

    def part(ref, k):
        return edges(lambda y: ref[y], k, per, shape)

    def body(h):
        for k in (2 * h, 2 * h + 1):
            payload[k] = joined(side, part(own_v, k), part(other_v, k), part(own_a, k))
        first, second = part(other_a, 2 * h), part(other_a, 2 * h + 1)
        payload[per + h] = jnp.where(window(side, 0, shape), first, turn(second, EDGE))

    each(per // 2, body, 2)


def pack_model_kernel(order, gathered, part, payload, model):
    peers, rows_own = gathered.shape[:2]
    per = model.shape[0] // GROUPS
    shape = gathered.shape[2:]
    side = facing()
    for i in range(peers):
        j = sum(((i >> n) & 1) << bit for n, bit in enumerate(order))
        model[pl.ds((lax.axis_index("src") ^ j) * rows_own, rows_own)] = gathered[i]
    packed = [edges(lambda y: model[y], k, per, shape) for k in range(per)]
    half = per // 2
    for h in range(half):
        payload[per + h] = jnp.where(window(side, -EDGE, shape), turn(packed[h], -EDGE), part[per + h])
    for n, k in enumerate(range(half, per, 3)):
        payload[per + half + n] = joined(side, *[packed[min(k + m, per - 1)] for m in range(3)])


def own_field_kernel(
    total_x, cells, means, variances, labels, own_model, model, warm, observed,
    scale, prior, main, main_2, b_m, b_r, measured, nothing,
):
    rows, depth, width = warm.shape
    shape = (depth, width)
    per = rows // GROUPS
    first_col = lax.axis_index("tile") * width
    nothing[...] = jnp.zeros(nothing.shape, F32)
    measured[...] = jnp.where(full(first_col, observed.shape) == 0, observed[...], 0.0)
    m = own_model[...]
    label = labels[...]
    mean_cell = jnp.zeros(m.shape, F32)
    var_cell = jnp.zeros(m.shape, F32)
    for cluster in range(CLUSTERS):
        mean_cell = jnp.where(label == cluster, means[cluster], mean_cell)
        var_cell = jnp.where(label == cluster, variances[cluster], var_cell)
    scale[...] = -jnp.exp(m)
    prior[...] = SMALLNESS * (m - mean_cell) / var_cell

    def body(k):
        for g in range(GROUPS):
            y = k + per * g
            r = k + (per + 2) * g
            shift = SLOT * g + HALF
            put_row(main, r, turn(warm[y], shift))
            put_row(main_2, r, turn(jnp.exp(model[y]), shift))
            b_m[y] = jnp.zeros(shape, F32)
        b_r[k] = jnp.zeros(shape, F32)

    each(per, body, 2)
    clear_ends(main, per)
    clear_ends(main_2, per)
    lane, depth_at = lane_of(shape), depth_of(shape)
    for n, sign in ((0, 1.0), (1, -1.0)):
        cell = cells[0, n]
        line = cell // total_x
        x = cell - line * total_x
        y = line // depth
        g = y // per
        k = y - g * per
        at_depth = depth_at == line - y * depth
        col_m = first_col + ((lane - (SLOT * g + HALF)) & 127)
        b_m[y] = b_m[y] + jnp.where((col_m == x) & at_depth, sign, 0.0)
        at_slot = (first_col + columns(GROUPS, shape) == x) & (lane // SLOT == g)
        b_r[k] = b_r[k] + jnp.where(at_slot & at_depth, sign, 0.0)


def turned_place(spots, first_col, width):
    x = spots[0:1, :] - first_col
    return jnp.where((x >= 0) & (x < width), (x + SLOT * spots[2:3, :] + HALF) & 127, -1)


def own_adjoint_kernel(mine, theirs, warm, spots, face_m, face_r, swept, swept_rim, hit_x, main, rim):
    rows, depth, width = warm.shape
    per = rows // GROUPS
    mask = window(1 - facing(), 0, (depth, width))

    def body(h):
        for n in range(2):
            k = 2 * h + n
            for g in range(GROUPS):
                put_row(main, k + (per + 2) * g, turn(warm[k + per * g], SLOT * g + HALF))
            far = turn(theirs[per + h], -EDGE * n)
            put_row(rim, k, jnp.where(mask, turn(mine[k], EDGE), far))

    each(per // 2, body, 1)
    clear_ends(main, per)
    clear_ends(swept, per)
    wrap(main, rim, per)
    sweep((main, rim), (swept, swept_rim), face_m, face_r, None, None, 0)
    first_col = lax.axis_index("tile") * width
    at = depth_of((width, spots.shape[1]))
    slot = at % SLOT
    rim_at = first_col + HALF - 1 - slot + jnp.where(slot < HALF, width, 0)
    hit_x[:width, :] = jnp.where(at == turned_place(spots, first_col, width), 1.0, 0.0).astype(BF16)
    hit_x[width:, :] = jnp.where(rim_at == spots[0:1, :], 1.0, 0.0).astype(BF16)


def save_kernel(field, adjoint, misfit, field_out, adjoint_out, misfit_out, plain_v, plain_a, sems):
    copies = [pltpu.make_async_copy(misfit, misfit_out, sems.at[2])]
    copies[0].start()
    rows = plain_v.shape[0]
    per = rows // GROUPS
    for n, (main, plain, out) in enumerate(((field, plain_v, field_out), (adjoint, plain_a, adjoint_out))):
        for y in range(rows):
            g = y // per
            plain[y] = turn(at_row(main, y + 2 * g), -(SLOT * g + HALF))
        copies.append(pltpu.make_async_copy(plain, out.at[0], sems.at[n]))
        copies[-1].start()
    for copy in copies:
        copy.wait()


def at_row(ref, y, shift=0):
    return ref[(y + 1) * DEPTH + shift : (y + 2) * DEPTH + shift, :]


def put_row(ref, y, values):
    start = (y + 1) * DEPTH
    if not isinstance(y, int):
        start = pl.multiple_of(start, DEPTH)
    ref[pl.ds(start, DEPTH), :] = values


def row_set(main, rim, k, per):
    return [at_row(main, g * (per + 2) + k) for g in range(GROUPS)] + [at_row(rim, k)]


def beside(own):
    packed = own[GROUPS]
    lane = lane_of(packed.shape)
    slot = lane % SLOT
    before, after = [], []
    for g in range(GROUPS):
        last = SLOT * g + HALF - 1
        after.append(jnp.where(lane == last, packed, turn(own[g], -1)))
        before.append(jnp.where(lane == last + 1, packed, turn(own[g], 1)))
    inner = merge(own[:GROUPS])
    before.append(jnp.where(slot == HALF - 1, inner, turn(packed, -1)))
    after.append(jnp.where(slot == HALF, inner, turn(packed, 1)))
    return before, after


def wrap(main, rim, per):
    put_row(rim, -1, turn(at_row(rim, per - 1), SLOT))
    put_row(rim, per, turn(at_row(rim, 0), -SLOT))
    for g in range(1, GROUPS):
        start = g * (per + 2)
        put_row(main, start - 1, turn(at_row(main, start - 3), SLOT))
        put_row(main, start - 2, turn(at_row(main, start), -SLOT))


def clear_ends(main, per):
    put_row(main, -1, jnp.zeros((DEPTH, main.shape[1]), F32))
    put_row(main, GROUPS * (per + 2) - 2, jnp.zeros((DEPTH, main.shape[1]), F32))


def sweep(old, new, face_m, face_r, b_m, b_r, first):
    per = face_r.shape[1] - 1
    for step in range(per):
        k = (first + step) % per
        if step == 0 or k == 0:
            above, own = row_set(*old, k - 1, per), row_set(*old, k, per)
            face_above = [face_m[2, (per + 1) * g + k] for g in range(GROUPS)] + [face_r[2, k]]
        else:
            above, own = own, below
        below = row_set(*old, k + 1, per)
        before, after = beside(own)
        done = []
        for g in range(GROUPS + 1):
            n = g // GROUPS
            face, b = ((face_m, face_r)[n], (b_m, b_r)[n])
            y = k if n else k + per * g
            r = k if n else k + (per + 2) * g
            c = k if n else k + (per + 1) * g
            fy, fz = face[2, c + 1], face[3, c + 1]
            total = face[0, c + 1] * after[g] + face[1, c + 1] * before[g]
            if b is not None:
                total = b[y] + total
            total = total + (fz * up_depth(own[g]) + down_depth(fz * own[g]))
            total = total + (fy * below[g] + face_above[g] * above[g])
            face_above[g] = fy
            done.append(total * face[4, c + 1])
            put_row(new[n], r, done[g])
        if k == 0:
            put_row(new[1], per, turn(done[GROUPS], -SLOT))
            for g in range(1, GROUPS):
                put_row(new[0], g * (per + 2) - 2, turn(done[g], -SLOT))
        if k == per - 1:
            put_row(new[1], -1, turn(done[GROUPS], SLOT))
            for g in range(1, GROUPS):
                put_row(new[0], g * (per + 2) - 1, turn(done[g - 1], SLOT))


def relax(first, second, face_m, face_r, b_m, b_r, start=0):
    per = face_r.shape[1] - 1
    clear_ends(second[0], per)
    wrap(*first, per)
    for n in range(start, SWEEPS):
        sweep(first, second, face_m, face_r, b_m, b_r, n)
        first, second = second, first
    return first


def three_parts(values):
    high = values.astype(BF16)
    rest = values - high.astype(F32)
    middle = rest.astype(BF16)
    low = (rest - middle.astype(F32)).astype(BF16)
    return high, middle, low


def columns(g, shape):
    if g == GROUPS:
        return rim_columns(shape, shape[1])
    return (lane_of(shape) - (SLOT * g + HALF)) & 127


def coefficients(total_x, first_col, main, rim, face_m, face_r):
    per = face_r.shape[1] - 1
    rows = per * GROUPS
    shape = face_r.shape[2:]
    group = lane_of(shape) // SLOT
    bottom = depth_of(shape) == shape[0] - 1
    for k in range(per):
        own = row_set(main, rim, k, per)
        before, after = beside(own)
        for g in range(GROUPS + 1):
            n = g // GROUPS
            field, face = ((main, rim)[n], (face_m, face_r)[n])
            y = k if n else k + per * g
            r = k if n else k + (per + 2) * g
            c = k if n else k + (per + 1) * g
            col = first_col + columns(g, shape)
            s = own[g]
            fx = jnp.where((col == total_x - 1) | (col == -1), 0.0, WEIGHT_X * 0.5 * (s + after[g]))
            bx = jnp.where((col == 0) | (col == total_x), 0.0, WEIGHT_X * 0.5 * (before[g] + s))
            fz = jnp.where(bottom, 0.0, WEIGHT_Z * 0.5 * (s + up_depth(s)))
            bz = down_depth(fz)
            fy = WEIGHT_Y * 0.5 * (s + at_row(field, r + 1))
            by = WEIGHT_Y * 0.5 * (at_row(field, r - 1) + s)
            if n and k == 0:
                by = jnp.where(group == 0, 0.0, by)
            if n and k == per - 1:
                fy = jnp.where(group == GROUPS - 1, 0.0, fy)
            if not n and y == 0:
                by = jnp.zeros(shape, F32)
            if not n and y == rows - 1:
                fy = jnp.zeros(shape, F32)
            diagonal = fx + bx + fy + by + fz + bz + LEAKAGE * s
            face[0, c + 1] = fx
            face[1, c + 1] = bx
            face[2, c + 1] = fy
            if not n and k == 0:
                face[2, c] = by
            face[3, c + 1] = fz
            face[4, c + 1] = 1.0 / diagonal
    face_r[2, 0] = turn(face_r[2, per], SLOT)


def field_kernel(
    total_x, mine, theirs, main_in, sigma_in, b_m, b_r, spots, measured,
    picked, main, rim, face_m, face_r, main_2, rim_2,
):
    del main_in, sigma_in
    rows, depth, width = b_m.shape
    shape = (depth, width)
    per = rows // GROUPS
    first_col = lax.axis_index("tile") * width
    mask = window(1 - facing(), 0, shape)
    filled = mask | window(facing(), 0, shape)
    for k in range(per):
        put_row(rim, k, jnp.where(mask, mine[k], turn(theirs[k], -EDGE)))
        row, offset = model_place(k, per)
        beyond = turn(jnp.where(window(1 - facing(), offset, shape), mine[row], theirs[row]), -offset)
        put_row(rim_2, k, jnp.exp(jnp.where(filled, beyond, 0.0)))
    wrap(main_2, rim_2, per)
    coefficients(total_x, first_col, main_2, rim_2, face_m, face_r)
    relax((main, rim), (main_2, rim_2), face_m, face_r, b_m, b_r)
    count = spots.shape[1]
    line_row = spots[1:2, :]
    place = turned_place(spots, first_col, width)
    hit_x = jnp.where(depth_of((width, count)) == place, 1.0, 0.0).astype(BF16)
    starts = [(g * (per + 2) + 1) * depth for g in range(GROUPS)]
    flat = jnp.concatenate([main[start : start + per * depth, :] for start in starts], axis=0)
    lines = sum(jnp.dot(part, hit_x, preferred_element_type=F32) for part in three_parts(flat))
    hit_line = depth_of((rows * depth, count)) == line_row
    got = jnp.sum(jnp.where(hit_line, lines, 0.0), axis=0, keepdims=True)
    picked[...] = got[:, : count // 2] - got[:, count // 2 :] - measured[...]


def adjoint_kernel(
    total_x, places, picked, spots, main_in, rim_in, hit_x, main_v, rim_v, face_m, face_r,
    terms, main_2, main_1, rim_1, rim_2, b_m, b_r,
):
    del main_in, rim_in
    rows, depth, width = b_m.shape
    shape = (depth, width)
    per = rows // GROUPS
    me = lax.axis_index("src")
    first_col = lax.axis_index("tile") * width
    count = spots.shape[1]
    misfit = picked[...]
    weights = jnp.concatenate([misfit, -misfit], axis=1)
    hit_line = depth_of((rows * depth, count)) == spots[1:2, :]
    flat = jnp.zeros((rows * depth, 2 * width), F32)
    for part in three_parts(weights):
        left = jnp.where(hit_line, part.astype(F32), 0.0).astype(BF16)
        flat = flat + lax.dot_general(left, hit_x[...], (((1,), (1,)), ((), ())), preferred_element_type=F32)
    flat = flat.reshape(rows, depth, 2 * width)
    for y in range(rows):
        b_m[y] = flat[y, :, :width]
    for k in range(per):
        b_r[k] = merge([flat[k + per * g, :, width:] for g in range(GROUPS)])
    for y in range(rows):
        r = y + 2 * (y // per)
        put_row(main_1, r, at_row(main_1, r) + b_m[y] * face_m[4, y + y // per + 1])
    for k in range(per):
        put_row(rim_1, k, at_row(rim_1, k) + b_r[k] * face_r[4, k + 1])
    main, rim = relax((main_1, rim_1), (main_2, rim_2), face_m, face_r, b_m, b_r, 1)
    rows_own = terms.shape[1]
    bottom = depth_of(shape) == depth - 1
    for k in range(per):
        f_own, a_own = row_set(main_v, rim_v, k, per), row_set(main, rim, k, per)
        f_before, f_after = beside(f_own)
        a_before, a_after = beside(a_own)
        for g in range(GROUPS):
            y, r = k + per * g, k + (per + 2) * g
            col = first_col + columns(g, shape)
            f, a = f_own[g], a_own[g]
            px_next = jnp.where(col == total_x - 1, 0.0, (f_after[g] - f) * (a_after[g] - a))
            px_prev = jnp.where(col == 0, 0.0, (f - f_before[g]) * (a - a_before[g]))
            py = jnp.zeros(shape, F32)
            if y + 1 < rows:
                py = py + (at_row(main_v, r + 1) - f) * (at_row(main, r + 1) - a)
            if y > 0:
                py = py + (f - at_row(main_v, r - 1)) * (a - at_row(main, r - 1))
            pz = jnp.where(bottom, 0.0, (at_row(main_v, r, 1) - f) * (at_row(main, r, 1) - a))
            pz = pz + down_depth(pz)
            paired = WEIGHT_X * (px_prev + px_next) + WEIGHT_Y * py + WEIGHT_Z * pz
            j = me ^ (y // rows_own)
            place = sum(((j >> bit) & 1) << n for n, bit in enumerate(reversed(places)))
            term = 0.5 * paired + LEAKAGE * f * a
            terms[place, y % rows_own] = turn(term, -(SLOT * g + HALF))


def gradient_kernel(scale, prior, kept, came, gradient):
    gradient[...] = scale[...] * (kept[...] + came[...]) + prior[...]


def on_device(
    log_conductivity,
    cluster_labels,
    cluster_means,
    cluster_vars,
    source_cells,
    receiver_cells,
    observed,
    warm_potential,
    warm_adjoint,
):
    tile, src = lax.axis_index("tile"), lax.axis_index("src")
    tiles, peers = lax.axis_size("tile"), lax.axis_size("src")
    rows_own, depth, width = log_conductivity.shape
    rows = rows_own * peers
    per = rows // GROUPS
    total_x = width * tiles
    receivers = receiver_cells.shape[0]
    bits = [1 << n for n in range(peers.bit_length() - 1)]
    levels = list(range(len(bits)))
    spots = receiver_cells.T.reshape(1, 2 * receivers)
    line = spots // total_x
    spots = jnp.concatenate([spots % total_x, line, line // (depth * per)], axis=0)
    spots = jnp.pad(spots, ((0, 5), (0, 0)), constant_values=-1)
    start_v, start_a = warm_potential[0], warm_adjoint[0]

    def shaped(*sizes):
        return jax.ShapeDtypeStruct(sizes, F32)

    other_v = lax.ppermute(start_v, "src", xor_pairs(peers, 1))
    other_a = lax.ppermute(start_a, "src", xor_pairs(peers, 1))
    order = levels[:0:-1] + [0]
    own = log_conductivity[None]
    gathered = lax.optimization_barrier(jnp.pad(own, ((0, peers - 1), (0, 0), (0, 0), (0, 0))))
    for n, level in enumerate(order):
        sent = own if n == 0 else gathered[: 1 << n]
        came = lax.ppermute(sent, "src", xor_pairs(peers, bits[level]))
        if n == PACK_AT:
            payload, gathered = pl.pallas_call(
                pack_fields_kernel,
                out_shape=(shaped(message_rows(per), depth, width), shaped(*gathered.shape)),
                in_specs=[VMEM] * 5,
                out_specs=(VMEM, VMEM),
                input_output_aliases={4: 1},
                cost_estimate=BESIDE,
                compiler_params=PARAMS,
            )(start_v, start_a, other_v, other_a, gathered)
        gathered = lax.dynamic_update_slice(gathered, came, (1 << n, 0, 0, 0))
    payload, model = pl.pallas_call(
        functools.partial(pack_model_kernel, order),
        out_shape=(shaped(*payload.shape), shaped(rows, depth, width)),
        in_specs=[VMEM, VMEM],
        out_specs=(VMEM, VMEM),
        input_output_aliases={1: 0},
        compiler_params=PARAMS,
    )(gathered, payload)
    pairs = []
    for t in range(tiles):
        for s in range(peers):
            t_to = (t + 1) % tiles if (t + s) % 2 == 0 else (t - 1) % tiles
            pairs.append((t * peers + s, t_to * peers + s))
    mine = lax.ppermute(payload, ("tile", "src"), pairs)
    main_shape, rim_shape = ((rows + 2 * GROUPS) * depth, width), ((per + 2) * depth, width)
    scale, prior, main_v, sigma, b_m, b_r, measured, nothing = pl.pallas_call(
        functools.partial(own_field_kernel, total_x),
        out_shape=(shaped(*log_conductivity.shape),) * 2
        + (shaped(*main_shape),) * 2
        + (
            shaped(rows, depth, width),
            shaped(per, depth, width),
            shaped(*observed.shape),
            shaped(1, depth, width),
        ),
        in_specs=[SMEM] * 3 + [VMEM] * 5,
        out_specs=(VMEM,) * 8,
        cost_estimate=BESIDE,
        compiler_params=PARAMS,
    )(
        source_cells, cluster_means, cluster_vars, cluster_labels, log_conductivity,
        model, start_v, observed,
    )
    theirs = lax.ppermute(mine + nothing, "src", xor_pairs(peers, 1))
    picked, main_v, rim_v, face_m, face_r, _ = pl.pallas_call(
        functools.partial(field_kernel, total_x),
        out_shape=(
            shaped(1, receivers),
            shaped(*main_shape),
            shaped(*rim_shape),
            shaped(5, rows + GROUPS, depth, width),
            shaped(5, per + 1, depth, width),
            shaped(*main_shape),
        ),
        in_specs=[VMEM] * 8,
        out_specs=(VMEM,) * 6,
        input_output_aliases={2: 1, 3: 5},
        scratch_shapes=[pltpu.VMEM(rim_shape, F32)],
        compiler_params=PARAMS,
    )(mine, theirs, main_v, sigma, b_m, b_r, spots, measured)
    main_a, rim_a, hit_x = pl.pallas_call(
        own_adjoint_kernel,
        out_shape=(
            shaped(*main_shape),
            shaped(*rim_shape),
            jax.ShapeDtypeStruct((2 * width, 2 * receivers), BF16),
        ),
        in_specs=[VMEM] * 6,
        out_specs=(VMEM,) * 3,
        scratch_shapes=[pltpu.VMEM(main_shape, F32), pltpu.VMEM(rim_shape, F32)],
        cost_estimate=BESIDE,
        compiler_params=PARAMS,
    )(mine, theirs, start_a, spots, face_m, face_r)

    step = 1
    while step < tiles:
        picked = picked + lax.ppermute(picked, "tile", xor_pairs(tiles, step))
        step *= 2

    terms, main_a, _, _ = pl.pallas_call(
        functools.partial(adjoint_kernel, total_x, levels),
        out_shape=(
            shaped(peers, rows_own, depth, width),
            shaped(*main_shape),
            shaped(*main_shape),
            shaped(*rim_shape),
        ),
        in_specs=[VMEM] * 9,
        out_specs=(VMEM,) * 4,
        input_output_aliases={2: 2, 3: 3},
        scratch_shapes=[
            pltpu.VMEM(rim_shape, F32),
            pltpu.VMEM((rows, depth, width), F32),
            pltpu.VMEM((per, depth, width), F32),
        ],
        compiler_params=PARAMS,
    )(picked, spots, main_a, rim_a, hit_x, main_v, rim_v, face_m, face_r)
    field, adjoint, misfit = pl.pallas_call(
        save_kernel,
        out_shape=(shaped(*warm_potential.shape), shaped(*warm_adjoint.shape), shaped(*observed.shape)),
        in_specs=[VMEM] * 3,
        out_specs=(HBM,) * 3,
        scratch_shapes=[pltpu.VMEM((rows, depth, width), F32)] * 2 + [pltpu.SemaphoreType.DMA((3,))],
        cost_estimate=BESIDE,
        compiler_params=PARAMS,
    )(main_v, main_a, picked)

    for level in levels[:-1]:
        keep = terms.shape[0] // 2
        terms = terms[:keep] + lax.ppermute(terms[keep:], "src", xor_pairs(peers, bits[level]))
    came = lax.ppermute(terms[1], "src", xor_pairs(peers, bits[-1]))
    gradient = pl.pallas_call(
        gradient_kernel,
        out_shape=shaped(*log_conductivity.shape),
        in_specs=[VMEM] * 4,
        out_specs=VMEM,
        compiler_params=PARAMS,
    )(scale, prior, terms[0], came)
    return (field, adjoint, misfit, gradient)


def solution(mesh):
    in_specs = (
        P("src", None, "tile"),
        P("src", None, "tile"),
        P(),
        P(),
        P("src", None),
        P(),
        P("src", None),
        P("src", None, None, "tile"),
        P("src", None, None, "tile"),
    )
    out_specs = (
        P("src", None, None, "tile"),
        P("src", None, None, "tile"),
        P("src", None),
        P("src", None, "tile"),
    )
    return jax.shard_map(
        on_device, mesh=mesh, in_specs=in_specs, out_specs=out_specs, check_vma=False
    )
```
